256 devices in a mesh: seq: 64 (over z, x, core), head: 4 (over y).
Axes of the slice: x: 4, y: 4, z: 8, core: 2. Of those that a mesh axis runs over, the one named last changes fastest.
Arguments:
- queries: bfloat16 [65536, 2048], P('seq', 'head'), may hold values from -5 to 5
- token_keys: bfloat16 [65536, 2048], P('seq', 'head'), may hold values from -5 to 5
- values: bfloat16 [65536, 2048], P('seq', 'head'), may hold values from -120 to 120
- norm_gain: float32 [2048], P('head'), may hold values from 0.25 to 1.75
- out_grad: bfloat16 [65536, 2048], P('seq', 'head'), may hold values from -6 to 6
Outputs:
- normed_out: bfloat16 [65536, 2048], P('seq', 'head')
- grad_queries: bfloat16 [65536, 2048], P('seq', 'head')
- grad_keys: bfloat16 [65536, 2048], P('seq', 'head')
- grad_values: bfloat16 [65536, 2048], P('seq', 'head')
The draws below stay inside these ranges and needn't reach their ends.
All inputs are finite; a program needn't handle non-finite values.
Results may differ from the reference program's by a relative error of at most 0.006.
Values sent between devices are 32-bit elements; how exact they have to be, the bound alone decides.
No kernel may reach another device: no remote copies, remote signals or barrier semaphores. Data moves between devices by JAX's collectives and lax.ppermute only.
A program may use at most 128 MiB of HBM per device.

```python
import math
import jax
import jax.numpy as jnp
from jax import lax

HEADS = 16
DK = 128
DV = 128
BLOCK = 512
TOKENS = 65536


def draw_values(key, part):
    key = jax.random.fold_in(key, 11)
    base_key, column_key = jax.random.split(key, 2)
    columns = HEADS * DV
    head_of = (jnp.arange(columns) // DV).astype(jnp.float32)
    head_scale = 3.0 ** (head_of / max(HEADS - 1, 1))
    column_scale = jnp.exp(jax.random.uniform(column_key, (columns,), jnp.float32, 0.0, math.log(10.0)))
    base = jnp.clip(jax.random.normal(base_key, (TOKENS, columns), jnp.float32), -4.0, 4.0)
    return (base * column_scale[None, :] * head_scale[None, :]).astype(jnp.bfloat16)


def steps_of(key, dims, cuts, low, top_value):
    def one(dim, shards_of):
        draws = jax.random.uniform(jax.random.fold_in(jax.random.fold_in(key, 6), dim), (shards_of,), jnp.float32, low / len(cuts), top_value / len(cuts))
        return jnp.repeat(jnp.exp(draws), dims[dim] // shards_of).reshape((-1,) + (1,) * (len(dims) - dim - 1))

    loudness = one(*cuts[0])
    for cut in cuts[1:]:
        loudness = loudness * one(*cut)
    return loudness


def normal_values(stream_key, dims, scale, most, cuts=(), kind=jnp.bfloat16):
    drawn = jax.random.normal(stream_key, dims, jnp.float32) * scale
    if len(cuts) > 0:
        drawn = steps_of(stream_key, dims, cuts, -0.22, 0.18) * drawn
    return jnp.clip(drawn, min=-most, max=most).astype(kind)


def setup_inputs(seed: int = 0) -> dict:
    streams_of = jax.random.split(jax.random.key(seed), 6)
    return {
        "queries": normal_values(streams_of[0], (TOKENS, HEADS * DK), 1.0, 5.0, ((0, 64), (1, 4))),
        "token_keys": normal_values(streams_of[1], (TOKENS, HEADS * DK), 1.0, 5.0, ((0, 64), (1, 4))),
        "values": draw_values(jax.random.fold_in(streams_of[5], 71), 0),
        "norm_gain": jnp.clip(1.0 + 0.15 * jax.random.normal(streams_of[3], (HEADS * DV,), jnp.float32), 0.25, 1.75),
        "out_grad": normal_values(streams_of[4], (TOKENS, HEADS * DV), 1.0, 6.0, ((0, 64), (1, 4))),
    }


def reference(queries, token_keys, values, norm_gain, out_grad):
    block_count = TOKENS // BLOCK
    query_blocks = queries.reshape(block_count, BLOCK, HEADS, DK)
    key_blocks = token_keys.reshape(block_count, BLOCK, HEADS, DK)
    value_blocks = values.reshape(block_count, BLOCK, HEADS, DV)
    position = jnp.arange(BLOCK, dtype=jnp.int32)
    causal = position[:, None] >= position[None, :]

    def masked_bf(matrix):
        return lax.optimization_barrier(jnp.where(causal[None], matrix, 0.0).astype(jnp.bfloat16))

    def forward_step(carry_state, blocks):
        query_now, key_now, value_now = blocks
        query_f = query_now.astype(jnp.float32)
        key_f = key_now.astype(jnp.float32)
        value_f = value_now.astype(jnp.float32)
        state_bf = lax.optimization_barrier(carry_state.astype(jnp.bfloat16))
        score_bf = masked_bf(jnp.einsum('thd,shd->hts', query_f, key_f))
        block_out = jnp.einsum('hts,she->the', score_bf.astype(jnp.float32), value_f)
        block_out = block_out + jnp.einsum('thd,hde->the', query_f, state_bf.astype(jnp.float32))
        carry_state = carry_state + jnp.einsum('thd,the->hde', key_f, value_f)
        return (carry_state, (block_out, state_bf))
    empty_state = jnp.zeros((HEADS, DK, DV), jnp.float32)
    _, (block_outs, prefix_bf) = lax.scan(forward_step, empty_state, (query_blocks, key_blocks, value_blocks))
    flat_out = block_outs.reshape(TOKENS, HEADS * DV)
    features = HEADS * DV
    root_mean = jnp.sqrt(lax.optimization_barrier(jnp.sum(flat_out * flat_out, axis=1, keepdims=True)) / features + 1e-05)
    normed_out = (norm_gain[None, :] * (flat_out / root_mean)).astype(jnp.bfloat16)
    scaled = norm_gain[None, :] * out_grad.astype(jnp.float32)
    inner_sum = lax.optimization_barrier(jnp.sum(flat_out * scaled, axis=1, keepdims=True))
    grad_attn = (scaled / root_mean - flat_out * inner_sum / (features * root_mean ** 3)).astype(jnp.bfloat16)
    grad_blocks = grad_attn.reshape(block_count, BLOCK, HEADS, DV)

    def backward_step(carry_state, blocks):
        query_now, key_now, value_now, grad_now, state_bf = blocks
        query_f = query_now.astype(jnp.float32)
        key_f = key_now.astype(jnp.float32)
        value_f = value_now.astype(jnp.float32)
        grad_f = grad_now.astype(jnp.float32)
        state_f = state_bf.astype(jnp.float32)
        suffix_bf = lax.optimization_barrier(carry_state.astype(jnp.bfloat16)).astype(jnp.float32)
        score_bf = masked_bf(jnp.einsum('thd,shd->hts', query_f, key_f)).astype(jnp.float32)
        grad_score = masked_bf(jnp.einsum('the,she->hts', grad_f, value_f)).astype(jnp.float32)
        grad_query = jnp.einsum('hts,shd->thd', grad_score, key_f) + jnp.einsum('the,hde->thd', grad_f, state_f)
        grad_key = jnp.einsum('hts,thd->shd', grad_score, query_f) + jnp.einsum('she,hde->shd', value_f, suffix_bf)
        grad_value = jnp.einsum('hts,the->she', score_bf, grad_f) + jnp.einsum('shd,hde->she', key_f, suffix_bf)
        carry_state = carry_state + jnp.einsum('thd,the->hde', query_f, grad_f)
        return (carry_state, (grad_query.astype(jnp.bfloat16), grad_key.astype(jnp.bfloat16), grad_value.astype(jnp.bfloat16)))
    _, (grad_q, grad_k, grad_v) = lax.scan(backward_step, empty_state, (query_blocks, key_blocks, value_blocks, grad_blocks, prefix_bf), reverse=True)
    return (normed_out, grad_q.reshape(TOKENS, HEADS * DK), grad_k.reshape(TOKENS, HEADS * DK), grad_v.reshape(TOKENS, HEADS * DV))
```

```python
import jax
import jax.numpy as jnp
from jax import lax
from jax.experimental import pallas as pl
from jax.experimental.pallas import tpu as pltpu
from jax.sharding import PartitionSpec as P

D = 128
BLOCK = 512
HALF = 256
F32 = jnp.float32
BF16 = jnp.bfloat16
PLANES, LINE, CORES = 8, 4, 2


def dot_nn(a, b):
    return lax.dot_general(a, b, (((1,), (0,)), ((), ())), preferred_element_type=F32)


def dot_nt(a, b):
    return lax.dot_general(a, b, (((1,), (1,)), ((), ())), preferred_element_type=F32)


def dot_tn(a, b):
    return lax.dot_general(a, b, (((0,), (0,)), ((), ())), preferred_element_type=F32)


def head_cols(h):
    return slice(h * D, (h + 1) * D)


def params(mib):
    return pltpu.CompilerParams(vmem_limit_bytes=mib * 2**20)


def lower(x):
    t = lax.broadcasted_iota(jnp.int32, x.shape, 0)
    s = lax.broadcasted_iota(jnp.int32, x.shape, 1)
    return jnp.where(t >= s, x, 0.0).astype(BF16)


def masked_product(left, right):
    top, bottom = slice(0, HALF), slice(HALF, BLOCK)
    full = dot_nt(left[bottom], right)
    first = lower(dot_nt(left[top], right[top]))
    return first, full[:, :HALF].astype(BF16), lower(full[:, HALF:])


def per_token(row):
    return jnp.transpose(jnp.broadcast_to(row, (D, row.shape[1])))


def places():
    me = lax.axis_index("seq")
    return me // (LINE * CORES), me // CORES % LINE, me % CORES


def shift(value, plane=0, line=0, swap=False):
    pairs = []
    for z in range(PLANES):
        for x in range(LINE):
            for c in range(CORES):
                source = (z * LINE + x) * CORES + c
                target = ((z + plane) % PLANES * LINE + (x + line) % LINE) * CORES + (1 - c if swap else c)
                pairs.append((source, target))
    return lax.ppermute(value, "seq", pairs)


def small(body, outs, rows, name, *args):
    vmem = pl.BlockSpec(memory_space=pltpu.VMEM)
    return pl.pallas_call(
        body,
        in_specs=[vmem] * len(args),
        out_specs=[vmem] * outs,
        out_shape=[jax.ShapeDtypeStruct((rows, D), F32)] * outs,
        compiler_params=params(4),
        name=name,
    )(*args)


def when(condition, value):
    return jnp.where(condition, value, 0.0)


def entering(mine, theirs, reverse):
    def ahead(other, me):
        return other > me if reverse else other < me

    half = mine.shape[0]
    piece = half // LINE
    partner = shift(theirs, swap=True)

    def split(mine, partner, *outs):
        _, x, _ = places()
        for k, out in enumerate(outs):
            at = pl.ds(pl.multiple_of((x + k) % LINE * piece, piece), piece)
            out[...] = mine[at] + partner[at]

    parts = small(split, LINE, piece, "split", mine, partner)
    parts = [parts[0]] + [shift(parts[k], line=k) for k in range(1, LINE)]

    def add(a, b, c, d, out):
        out[...] = a[...] + b[...] + c[...] + d[...]

    (plane,) = small(add, 1, piece, "add", *parts)
    below, above = shift(plane, plane=1), shift(plane, plane=-1)

    def windows(plane, below, above, to_up, to_down):
        z, _, _ = places()
        before, after = (z + PLANES - 1) % PLANES, (z + 1) % PLANES
        up, down = (z + 3) % PLANES, (z + PLANES - 3) % PLANES
        to_up[...] = (
            when(ahead(before, up), below[...]) + when(ahead(z, up), plane[...]) + when(ahead(after, up), above[...])
        )
        to_down[...] = when(ahead(before, down), below[...]) + when(ahead(z, down), plane[...])

    to_up, to_down = small(windows, 2, piece, "windows", plane, below, above)
    from_down, from_up = shift(to_up, plane=3), shift(to_down, plane=-3)

    def spread(below, above, from_down, from_up, *refs):
        parts, outs = refs[:LINE], refs[LINE:]
        z, x, _ = places()
        before, after = (z + PLANES - 1) % PLANES, (z + 1) % PLANES
        planes = (
            when(ahead(before, z), below[...]) + when(ahead(after, z), above[...]) + from_down[...] + from_up[...]
        )
        for j, out in enumerate(outs):
            target = (x + j) % LINE
            total = planes
            for k, part in enumerate(parts):
                total += when(ahead((x + LINE - k) % LINE, target), part[...])
            out[...] = total

    sent = small(spread, LINE, piece, "spread", below, above, from_down, from_up, *parts)
    got = [sent[0]] + [shift(sent[j], line=j) for j in range(1, LINE)]

    def collect(mine, partner, *refs):
        got, (kept, other) = refs[:LINE], refs[LINE:]
        _, x, c = places()
        for k, part in enumerate(got):
            at = pl.ds(pl.multiple_of((x + LINE - k) % LINE * piece, piece), piece)
            kept[at] = part[...] + when(ahead(1 - c, c), partner[at])
            other[at] = part[...] + when(ahead(c, 1 - c), mine[at])

    kept, other = small(collect, 2, half, "collect", mine, partner, *got)
    return kept, shift(other, swap=True)


def state_of(h, kept, other):
    _, _, c = places()
    heads = kept.shape[0] // D
    at = slice(h % heads * D, (h % heads + 1) * D)
    return jnp.where(c == h // heads, kept[at], other[at])


def products(left, right):
    width = left.shape[1]
    heads = width // D

    def body(a, b, first, mine, theirs):
        h = pl.program_id(0)
        _, _, c = places()
        one = dot_tn(a[:BLOCK], b[:BLOCK])
        total = one + dot_tn(a[BLOCK:], b[BLOCK:])
        first[...] = one
        at = pl.ds(pl.multiple_of(h % (heads // CORES) * D, D), D)

        @pl.when(h // (heads // CORES) == c)
        def _():
            mine[at] = total

        @pl.when(h // (heads // CORES) != c)
        def _():
            theirs[at] = total

    column = pl.BlockSpec((2 * BLOCK, D), lambda h: (0, h))
    half = pl.BlockSpec((width // CORES, D), lambda h: (0, 0))
    half_shape = jax.ShapeDtypeStruct((width // CORES, D), F32)
    return pl.pallas_call(
        body,
        grid=(heads,),
        in_specs=[column, column],
        out_specs=[pl.BlockSpec((D, D), lambda h: (h, 0)), half, half],
        out_shape=[jax.ShapeDtypeStruct((width, D), F32), half_shape, half_shape],
        compiler_params=params(8),
        name="products",
    )(left, right)


def local_attention(q, k, v, heads, first_head, cost=True):
    length = q.shape[0]

    def body(q, k, v, out):
        qv, kv, vv = q[...], k[...], v[...]
        a, b, c = masked_product(qv, kv)
        out[:HALF] = dot_nn(a, vv[:HALF])
        out[HALF:] = dot_nn(b, vv[:HALF]) + dot_nn(c, vv[HALF:])

    spec = pl.BlockSpec((BLOCK, D), lambda c, h: (c, first_head + h))
    return pl.pallas_call(
        body,
        grid=(length // BLOCK, heads),
        in_specs=[spec, spec, spec],
        out_specs=pl.BlockSpec((BLOCK, D), lambda c, h: (c, h)),
        out_shape=jax.ShapeDtypeStruct((length, heads * D), F32),
        compiler_params=params(8),
        cost_estimate=pl.CostEstimate(
            flops=length // BLOCK * heads * 4 * BLOCK * BLOCK * D,
            bytes_accessed=length * heads * D * 10,
            transcendentals=0,
        ),
        name="local_attention",
    )(q, k, v)


def attention_sums(q, grad, local, gain, kept, other, first):
    length, width = q.shape
    heads = width // D

    def body(q, grad, local, gain, kept, other, first, attn, sums):
        later = (pl.program_id(0) > 0).astype(F32)
        square = jnp.zeros((BLOCK, D), F32)
        inner = jnp.zeros((BLOCK, D), F32)
        for h in range(heads):
            cols = head_cols(h)
            prefix = (state_of(h, kept, other) + later * first[cols]).astype(BF16)
            a = local[:, cols] + dot_nn(q[:, cols], prefix)
            attn[:, cols] = a
            square += a * a
            inner += a * (gain[:, cols] * grad[:, cols].astype(F32))
        sums[0:1] = jnp.sum(jnp.transpose(square), axis=0, keepdims=True)
        sums[1:2] = jnp.sum(jnp.transpose(inner), axis=0, keepdims=True)

    rows = pl.BlockSpec((BLOCK, width), lambda c: (c, 0))
    whole = pl.BlockSpec((width, D), lambda c: (0, 0))
    half = pl.BlockSpec((width // CORES, D), lambda c: (0, 0))
    return pl.pallas_call(
        body,
        grid=(length // BLOCK,),
        in_specs=[rows, rows, rows, pl.BlockSpec((1, width), lambda c: (0, 0)), half, half, whole],
        out_specs=[rows, pl.BlockSpec((2, BLOCK), lambda c: (0, c))],
        out_shape=[
            jax.ShapeDtypeStruct((length, width), F32),
            jax.ShapeDtypeStruct((2, length), F32),
        ],
        compiler_params=params(12),
        name="attention_sums",
    )(q, grad, local, gain, kept, other, first)


def token_scales(sums, features):
    root = jnp.sqrt(sums[0:1] / features + 1e-05)
    inverse = 1.0 / root
    weight = sums[1:2] / (features * root**3)
    return per_token(inverse), per_token(weight)


def gradient(q, grad, attn, gain, sums, features):
    length, width = q.shape
    heads = width // D
    per_core = heads // CORES

    def body(q, grad, attn, gain, sums, out, last, mine, theirs):
        step = pl.program_id(0)
        _, _, c = places()
        inverse, weight = token_scales(sums[...], features)
        for h in range(heads):
            cols = head_cols(h)
            scaled = gain[:, cols] * grad[:, cols].astype(F32)
            g = (scaled * inverse - attn[:, cols] * weight).astype(BF16)
            out[:, cols] = g
            term = dot_tn(q[:, cols], g)
            last[cols] = term
            at = head_cols(h % per_core)
            for owned, half in ((c, mine), (1 - c, theirs)):

                @pl.when((owned == h // per_core) & (step == 0))
                def _(half=half):
                    half[at] = term

                @pl.when((owned == h // per_core) & (step > 0))
                def _(half=half):
                    half[at] += term

    rows = pl.BlockSpec((BLOCK, width), lambda c: (c, 0))
    whole = pl.BlockSpec((width, D), lambda c: (0, 0))
    half = pl.BlockSpec((width // CORES, D), lambda c: (0, 0))
    half_shape = jax.ShapeDtypeStruct((width // CORES, D), F32)
    return pl.pallas_call(
        body,
        grid=(length // BLOCK,),
        in_specs=[
            rows,
            rows,
            rows,
            pl.BlockSpec((1, width), lambda c: (0, 0)),
            pl.BlockSpec((2, BLOCK), lambda c: (0, c)),
        ],
        out_specs=[rows, whole, half, half],
        out_shape=[
            jax.ShapeDtypeStruct((length, width), BF16),
            jax.ShapeDtypeStruct((width, D), F32),
            half_shape,
            half_shape,
        ],
        compiler_params=params(12),
        name="gradient",
    )(q, grad, attn, gain, sums)


def local_gradients(q, k, v, g, attn, gain, sums, kept, other, first, features):
    length, width = q.shape
    heads = width // D
    per_core = heads // CORES

    def body(q, k, v, g, attn, gain, sums, kept, other, first, normed, dq, dk, dv):
        later = (pl.program_id(0) > 0).astype(F32)
        root = jnp.sqrt(sums[0:1] / features + 1e-05)
        normed[...] = (gain[...] * (attn[...] * per_token(1.0 / root))).astype(BF16)
        h = pl.program_id(1)
        _, _, core = places()
        at = pl.ds(pl.multiple_of(h % per_core * D, D), D)
        state = jnp.where(core == h // per_core, kept[at], other[at])
        prefix = (state + later * first[...]).astype(BF16)
        top, bottom = slice(0, HALF), slice(HALF, BLOCK)
        qv, kv, vv, gv = q[...], k[...], v[...], g[...]
        a, b, c = masked_product(gv, vv)
        carried = dot_nt(gv, prefix)
        dq[top] = (dot_nn(a, kv[top]) + carried[top]).astype(BF16)
        dq[bottom] = (dot_nn(b, kv[top]) + dot_nn(c, kv[bottom]) + carried[bottom]).astype(BF16)
        dk[top] = dot_tn(a, qv[top]) + dot_tn(b, qv[bottom])
        dk[bottom] = dot_tn(c, qv[bottom])
        a, b, c = masked_product(qv, kv)
        dv[top] = dot_tn(a, gv[top]) + dot_tn(b, gv[bottom])
        dv[bottom] = dot_tn(c, gv[bottom])

    tile = pl.BlockSpec((BLOCK, D), lambda c, h: (c, h))
    one = pl.BlockSpec((D, D), lambda c, h: (h, 0))
    half = pl.BlockSpec((width // CORES, D), lambda c, h: (0, 0))
    return pl.pallas_call(
        body,
        grid=(length // BLOCK, heads),
        in_specs=[tile] * 5
        + [
            pl.BlockSpec((1, D), lambda c, h: (0, h)),
            pl.BlockSpec((2, BLOCK), lambda c, h: (0, c)),
            half,
            half,
            one,
        ],
        out_specs=[tile] * 4,
        out_shape=[jax.ShapeDtypeStruct((length, width), t) for t in (BF16, BF16, F32, F32)],
        compiler_params=params(12),
        cost_estimate=pl.CostEstimate(
            flops=length // BLOCK * heads * 10 * BLOCK * BLOCK * D,
            bytes_accessed=length * width * 24,
            transcendentals=0,
        ),
        name="local_gradients",
    )(q, k, v, g, attn, gain, sums, kept, other, first)


def add_suffix(k, v, dk, dv, kept, other, last):
    length, width = k.shape
    heads = width // D
    rows_of = HALF

    def body(k, v, dk, dv, kept, other, last, out_k, out_v):
        earlier = (pl.program_id(0) < BLOCK // rows_of).astype(F32)
        for h in range(heads):
            cols = head_cols(h)
            suffix = (state_of(h, kept, other) + earlier * last[cols]).astype(BF16)
            out_k[:, cols] = (dk[:, cols] + dot_nt(v[:, cols], suffix)).astype(BF16)
            out_v[:, cols] = (dv[:, cols] + dot_nn(k[:, cols], suffix)).astype(BF16)

    rows = pl.BlockSpec((rows_of, width), lambda c: (c, 0))
    whole = pl.BlockSpec((width, D), lambda c: (0, 0))
    half = pl.BlockSpec((width // CORES, D), lambda c: (0, 0))
    shape = jax.ShapeDtypeStruct((length, width), BF16)
    return pl.pallas_call(
        body,
        grid=(length // rows_of,),
        in_specs=[rows, rows, rows, rows, half, half, whole],
        out_specs=[rows, rows],
        out_shape=[shape, shape],
        compiler_params=params(12),
        name="add_suffix",
    )(k, v, dk, dv, kept, other, last)


def head_sum(part):
    count = lax.axis_size("head")
    total = part
    for k in range(1, count):
        total = total + lax.ppermute(part, "head", [(i, (i + k) % count) for i in range(count)])
    return total


def on_device(queries, token_keys, values, norm_gain, out_grad):
    heads = queries.shape[1] // D
    features = lax.axis_size("head") * heads * D
    gain = norm_gain.reshape(1, heads * D)
    first, mine, theirs = products(token_keys, values)
    local = local_attention(queries, token_keys, values, heads, 0)
    kept, other = entering(mine, theirs, False)
    attn, sums = attention_sums(queries, out_grad, local, gain, kept, other, first)
    sums = head_sum(sums)
    grad_attn, last, mine, theirs = gradient(queries, out_grad, attn, gain, sums, features)
    normed_out, grad_query, key_part, value_part = local_gradients(
        queries, token_keys, values, grad_attn, attn, gain, sums, kept, other, first, features
    )
    kept, other = entering(mine, theirs, True)
    grad_key, grad_value = add_suffix(token_keys, values, key_part, value_part, kept, other, last)
    return normed_out, grad_query, grad_key, grad_value


def solution(mesh):
    placed = (P("seq", "head"), P("seq", "head"), P("seq", "head"), P("head"), P("seq", "head"))
    return jax.shard_map(
        on_device,
        mesh=mesh,
        in_specs=placed,
        out_specs=(P("seq", "head"), P("seq", "head"), P("seq", "head"), P("seq", "head")),
        check_vma=False,
    )
```

```python
import jax
import jax.numpy as jnp
from jax import lax
from jax.experimental import pallas as pl
from jax.experimental.pallas import tpu as pltpu
from jax.sharding import PartitionSpec as P

D = 128
BLOCK = 512
HALF = 256
F32 = jnp.float32
BF16 = jnp.bfloat16
PLANES, LINE, CORES = 8, 4, 2


def dot_nn(a, b):
    return lax.dot_general(a, b, (((1,), (0,)), ((), ())), preferred_element_type=F32)


def dot_nt(a, b):
    return lax.dot_general(a, b, (((1,), (1,)), ((), ())), preferred_element_type=F32)


def dot_tn(a, b):
    return lax.dot_general(a, b, (((0,), (0,)), ((), ())), preferred_element_type=F32)


def head_cols(h):
    return slice(h * D, (h + 1) * D)


def params(mib):
    return pltpu.CompilerParams(vmem_limit_bytes=mib * 2**20)


def lower(x):
    t = lax.broadcasted_iota(jnp.int32, x.shape, 0)
    s = lax.broadcasted_iota(jnp.int32, x.shape, 1)
    return jnp.where(t >= s, x, 0.0).astype(BF16)


def upper(x):
    s = lax.broadcasted_iota(jnp.int32, x.shape, 0)
    t = lax.broadcasted_iota(jnp.int32, x.shape, 1)
    return jnp.where(t >= s, x, 0.0).astype(BF16)


TOP, BOTTOM = slice(0, HALF), slice(HALF, BLOCK)
VMEM = pl.BlockSpec(memory_space=pltpu.VMEM)
HBM = pl.BlockSpec(memory_space=pltpu.HBM)
ANY = pl.BlockSpec(memory_space=pl.ANY)


def lower_product(left, right):
    full = dot_nt(left[BOTTOM], right)
    first = lower(dot_nt(left[TOP], right[TOP]))
    return first, full[:, :HALF].astype(BF16), lower(full[:, HALF:])


def upper_product(left, right):
    full = dot_nt(left[TOP], right)
    last = upper(dot_nt(left[BOTTOM], right[BOTTOM]))
    return upper(full[:, :HALF]), full[:, HALF:].astype(BF16), last


def per_token(row):
    return jnp.transpose(jnp.broadcast_to(row, (D, row.shape[1])))


def beside(a, b):
    return jnp.concatenate([a, b], axis=1)


def block_rows(c):
    return slice(c * BLOCK, (c + 1) * BLOCK)


def places():
    me = lax.axis_index("seq")
    return me // (LINE * CORES), me // CORES % LINE, me % CORES


def shift(value, plane=0, line=0, swap=False):
    pairs = []
    for z in range(PLANES):
        for x in range(LINE):
            for c in range(CORES):
                source = (z * LINE + x) * CORES + c
                target = ((z + plane) % PLANES * LINE + (x + line) % LINE) * CORES + (1 - c if swap else c)
                pairs.append((source, target))
    return lax.ppermute(value, "seq", pairs)


def small(body, outs, rows, name, args, after=()):
    def waiting(*refs):
        body(*refs[: len(args)], *refs[len(args) + len(after) :])

    return pl.pallas_call(
        waiting,
        in_specs=[VMEM] * len(args) + [ANY] * len(after),
        out_specs=[VMEM] * outs,
        out_shape=[jax.ShapeDtypeStruct((rows, D), F32)] * outs,
        compiler_params=params(4),
        name=name,
    )(*args, *after)


def when(condition, value):
    return jnp.where(condition, value, 0.0)


def entering(mine, theirs, reverse, beside_rounds):
    def ahead(other, me):
        return other > me if reverse else other < me

    half = mine.shape[0]
    piece = half // LINE
    partner = shift(theirs, swap=True)

    def split(mine, partner, *outs):
        _, x, _ = places()
        for k, out in enumerate(outs):
            at = pl.ds(pl.multiple_of((x + k) % LINE * piece, piece), piece)
            out[...] = mine[at] + partner[at]

    parts = small(split, LINE, piece, "split", (mine, partner))
    done = beside_rounds[0](parts[0])
    parts = [parts[0]] + [shift(parts[k], line=k) for k in range(1, LINE)]

    def add(a, b, c, d, out):
        out[...] = a[...] + b[...] + c[...] + d[...]

    (plane,) = small(add, 1, piece, "add", parts, done)
    done = beside_rounds[1](plane)
    below, above = shift(plane, plane=1), shift(plane, plane=-1)

    def windows(plane, below, above, to_up, to_down):
        z, _, _ = places()
        before, after = (z + PLANES - 1) % PLANES, (z + 1) % PLANES
        up, down = (z + 3) % PLANES, (z + PLANES - 3) % PLANES
        to_up[...] = (
            when(ahead(before, up), below[...]) + when(ahead(z, up), plane[...]) + when(ahead(after, up), above[...])
        )
        to_down[...] = when(ahead(before, down), below[...]) + when(ahead(z, down), plane[...])

    to_up, to_down = small(windows, 2, piece, "windows", (plane, below, above), done)
    done = beside_rounds[2](to_up)
    from_down, from_up = shift(to_up, plane=3), shift(to_down, plane=-3)

    def spread(below, above, from_down, from_up, *refs):
        parts, outs = refs[:LINE], refs[LINE:]
        z, x, _ = places()
        before, after = (z + PLANES - 1) % PLANES, (z + 1) % PLANES
        planes = (
            when(ahead(before, z), below[...]) + when(ahead(after, z), above[...]) + from_down[...] + from_up[...]
        )
        for j, out in enumerate(outs):
            target = (x + j) % LINE
            total = planes
            for k, part in enumerate(parts):
                total += when(ahead((x + LINE - k) % LINE, target), part[...])
            out[...] = total

    sent = small(spread, LINE, piece, "spread", (below, above, from_down, from_up, *parts), done)
    done = beside_rounds[3](sent[0])
    got = [sent[0]] + [shift(sent[j], line=j) for j in range(1, LINE)]

    def collect(mine, partner, *refs):
        got, (kept, other) = refs[:LINE], refs[LINE:]
        _, x, c = places()
        for k, part in enumerate(got):
            at = pl.ds(pl.multiple_of((x + LINE - k) % LINE * piece, piece), piece)
            kept[at] = part[...] + when(ahead(1 - c, c), partner[at])
            other[at] = part[...] + when(ahead(c, 1 - c), mine[at])

    kept, other = small(collect, 2, half, "collect", (mine, partner, *got), done)
    return kept, shift(other, swap=True)


def state_of(h, kept, other):
    _, _, c = places()
    heads = kept.shape[0] // D
    at = slice(h % heads * D, (h % heads + 1) * D)
    return jnp.where(c == h // heads, kept[at], other[at])


def products(left, right):
    length, width = left.shape
    heads = width // D
    blocks = length // BLOCK
    per_core = heads // CORES

    def body(left_hbm, right_hbm, left, right, first, mine, theirs, sems):
        copies = []
        for c in range(blocks):
            rows = pl.ds(c * BLOCK, BLOCK)
            pair = [
                pltpu.make_async_copy(left_hbm.at[rows], left.at[rows], sems.at[0, c]),
                pltpu.make_async_copy(right_hbm.at[rows], right.at[rows], sems.at[1, c]),
            ]
            for copy in pair:
                copy.start()
            copies.append(pair)
        total = [None] * heads
        for c in range(blocks):
            for copy in copies[c]:
                copy.wait()
            for h in range(heads):
                term = dot_tn(left[block_rows(c), head_cols(h)], right[block_rows(c), head_cols(h)])
                if c == 0:
                    first[head_cols(h)] = term
                total[h] = term if c == 0 else total[h] + term
        _, _, core = places()
        for h in range(heads):
            store_half(core, h, per_core, total[h], mine, theirs)

    half_shape = jax.ShapeDtypeStruct((width // CORES, D), F32)
    return pl.pallas_call(
        body,
        in_specs=[HBM, HBM],
        out_specs=[VMEM] * 5,
        out_shape=[
            jax.ShapeDtypeStruct(left.shape, BF16),
            jax.ShapeDtypeStruct(right.shape, BF16),
            jax.ShapeDtypeStruct((width, D), F32),
            half_shape,
            half_shape,
        ],
        scratch_shapes=[pltpu.SemaphoreType.DMA((2, blocks))],
        compiler_params=params(12),
        name="products",
    )(pltpu.with_memory_space_constraint(left, pltpu.HBM), pltpu.with_memory_space_constraint(right, pltpu.HBM))


def store_half(core, h, per_core, value, mine, theirs):
    at = head_cols(h % per_core)

    @pl.when(core == h // per_core)
    def _():
        mine[at] = value

    @pl.when(core != h // per_core)
    def _():
        theirs[at] = value


def local_attention(q, k, v, h, after):
    length = q.shape[0]

    def body(q, k, v, _, out):
        for c in range(length // BLOCK):
            rows = block_rows(c)
            qv, kv, vv = (x[rows, head_cols(h)] for x in (q, k, v))
            a, b, d = lower_product(qv, kv)
            out[c * BLOCK : c * BLOCK + HALF] = dot_nn(a, vv[TOP])
            out[c * BLOCK + HALF : (c + 1) * BLOCK] = dot_nn(beside(b, d), vv)

    return pl.pallas_call(
        body,
        in_specs=[VMEM, VMEM, VMEM, ANY],
        out_specs=VMEM,
        out_shape=jax.ShapeDtypeStruct((length, D), F32),
        compiler_params=params(12),
        cost_estimate=pl.CostEstimate(
            flops=length // BLOCK * 4 * BLOCK * BLOCK * D, bytes_accessed=length * D * 10, transcendentals=0
        ),
        name="local_attention",
    )(q, k, v, after)


def attention_sums(q, grad, local, gain, kept, other, first):
    length, width = q.shape
    heads = width // D

    def body(q, grad, *refs):
        local, (gain, kept, other, first, attn, sums) = refs[:heads], refs[heads:]
        for c in range(length // BLOCK):
            rows = block_rows(c)
            square = jnp.zeros((BLOCK, D), F32)
            inner = jnp.zeros((BLOCK, D), F32)
            for h in range(heads):
                cols = head_cols(h)
                prefix = state_of(h, kept, other)
                if c > 0:
                    prefix += first[cols]
                a = local[h][rows] + dot_nn(q[rows, cols], prefix.astype(BF16))
                attn[rows, cols] = a
                square += a * a
                inner += a * (gain[:, cols] * grad[rows, cols].astype(F32))
            sums[0:1, rows] = jnp.sum(jnp.transpose(square), axis=0, keepdims=True)
            sums[1:2, rows] = jnp.sum(jnp.transpose(inner), axis=0, keepdims=True)

    return pl.pallas_call(
        body,
        in_specs=[VMEM] * (6 + heads),
        out_specs=[VMEM] * 2,
        out_shape=[
            jax.ShapeDtypeStruct((length, width), F32),
            jax.ShapeDtypeStruct((2, length), F32),
        ],
        compiler_params=params(16),
        name="attention_sums",
    )(q, grad, *local, gain, kept, other, first)


def gradient(q, grad, attn, gain, sums, features):
    length, width = q.shape
    heads = width // D
    blocks = length // BLOCK

    def body(q, grad, attn, gain, sums, out, last, mine, theirs):
        total = [None] * heads
        for c in range(blocks):
            rows = block_rows(c)
            root = jnp.sqrt(sums[0:1, rows] / features + 1e-05)
            inverse = per_token(1.0 / root)
            weight = per_token(sums[1:2, rows] / (features * root**3))
            for h in range(heads):
                cols = head_cols(h)
                scaled = gain[:, cols] * grad[rows, cols].astype(F32)
                g = (scaled * inverse - attn[rows, cols] * weight).astype(BF16)
                out[rows, cols] = g
                term = dot_tn(q[rows, cols], g)
                total[h] = term if c == 0 else total[h] + term
                if c == blocks - 1:
                    last[cols] = term
        _, _, core = places()
        for h in range(heads):
            store_half(core, h, heads // CORES, total[h], mine, theirs)

    half_shape = jax.ShapeDtypeStruct((width // CORES, D), F32)
    return pl.pallas_call(
        body,
        in_specs=[VMEM] * 5,
        out_specs=[VMEM] * 4,
        out_shape=[
            jax.ShapeDtypeStruct((length, width), BF16),
            jax.ShapeDtypeStruct((width, D), F32),
            half_shape,
            half_shape,
        ],
        compiler_params=params(16),
        name="gradient",
    )(q, grad, attn, gain, sums)


def local_gradients(q, k, v, g, attn, gain, sums, kept, other, first, features, h, outs, after):
    length, width = q.shape
    blocks = length // BLOCK
    cols = head_cols(h)

    def body(q, k, v, g, attn, gain, sums, kept, other, first, *refs):
        normed, dq, dk, dv, normed_here, dq_here, sems = refs[len(outs) + 1 :]
        copies = []

        def send(here, out, i, c):
            copy = pltpu.make_async_copy(here.at[block_rows(c)], out.at[block_rows(c), cols], sems.at[i, c])
            copy.start()
            copies.append(copy)

        state = state_of(h, kept, other)
        for c in range(blocks):
            rows = block_rows(c)
            root = jnp.sqrt(sums[0:1, rows] / features + 1e-05)
            normed_here[rows] = (gain[:, cols] * (attn[rows, cols] * per_token(1.0 / root))).astype(BF16)
            send(normed_here, normed, 0, c)
            qv, kv, vv, gv = (x[rows, cols] for x in (q, k, v, g))
            prefix = state + first[cols] if c > 0 else state
            carried = dot_nt(gv, prefix.astype(BF16))
            a, b, d = lower_product(gv, vv)
            top, bottom = slice(c * BLOCK, c * BLOCK + HALF), slice(c * BLOCK + HALF, (c + 1) * BLOCK)
            dq_here[top] = (dot_nn(a, kv[TOP]) + carried[TOP]).astype(BF16)
            dq_here[bottom] = (dot_nn(beside(b, d), kv) + carried[BOTTOM]).astype(BF16)
            send(dq_here, dq, 1, c)
            a, b, d = upper_product(vv, gv)
            dk[top] = dot_nn(beside(a, b), qv)
            dk[bottom] = dot_nn(d, qv[BOTTOM])
            a, b, d = upper_product(kv, qv)
            dv[top] = dot_nn(beside(a, b), gv)
            dv[bottom] = dot_nn(d, gv[BOTTOM])
        for copy in copies:
            copy.wait()

    return pl.pallas_call(
        body,
        in_specs=[VMEM] * 10 + [HBM] * len(outs) + [ANY],
        out_specs=[HBM, HBM, VMEM, VMEM],
        out_shape=[jax.ShapeDtypeStruct((length, width), BF16)] * 2 + [jax.ShapeDtypeStruct((length, D), F32)] * 2,
        scratch_shapes=[pltpu.VMEM((length, D), BF16)] * 2 + [pltpu.SemaphoreType.DMA((2, blocks))],
        input_output_aliases={10 + i: i for i in range(len(outs))},
        compiler_params=params(20),
        cost_estimate=pl.CostEstimate(
            flops=blocks * 12 * BLOCK * BLOCK * D, bytes_accessed=length * D * 20, transcendentals=0
        ),
        name="local_gradients",
    )(q, k, v, g, attn, gain, sums, kept, other, first, *outs, after)


def add_suffix(k, v, dk, dv, kept, other, last):
    length, width = k.shape
    heads = width // D
    steps = length // HALF

    def body(k, v, *refs):
        dk, dv = refs[:heads], refs[heads : 2 * heads]
        kept, other, last, out_k, out_v, here_k, here_v, sems = refs[2 * heads :]
        copies = []
        for i in range(steps):
            rows = slice(i * HALF, (i + 1) * HALF)
            for h in range(heads):
                cols = head_cols(h)
                suffix = state_of(h, kept, other)
                if (i + 1) * HALF <= length - BLOCK:
                    suffix += last[cols]
                suffix = suffix.astype(BF16)
                here_k[rows, cols] = (dk[h][rows] + dot_nt(v[rows, cols], suffix)).astype(BF16)
                here_v[rows, cols] = (dv[h][rows] + dot_nn(k[rows, cols], suffix)).astype(BF16)
            for here, out, j in ((here_k, out_k, 0), (here_v, out_v, 1)):
                copy = pltpu.make_async_copy(here.at[rows], out.at[rows], sems.at[j, i])
                copy.start()
                copies.append(copy)
        for copy in copies:
            copy.wait()

    shape = jax.ShapeDtypeStruct((length, width), BF16)
    return pl.pallas_call(
        body,
        in_specs=[VMEM] * (5 + 2 * heads),
        out_specs=[HBM, HBM],
        out_shape=[shape, shape],
        scratch_shapes=[pltpu.VMEM((length, width), BF16)] * 2 + [pltpu.SemaphoreType.DMA((2, steps))],
        compiler_params=params(16),
        name="add_suffix",
    )(k, v, *dk, *dv, kept, other, last)


def head_sum(part):
    count = lax.axis_size("head")
    total = part
    for k in range(1, count):
        total = total + lax.ppermute(part, "head", [(i, (i + k) % count) for i in range(count)])
    return total


def on_device(queries, token_keys, values, norm_gain, out_grad):
    heads = queries.shape[1] // D
    features = lax.axis_size("head") * heads * D
    gain = norm_gain.reshape(1, heads * D)
    keys, vals, first, mine, theirs = products(token_keys, values)
    local = []

    def attend(h):
        def run(after):
            local.append(local_attention(queries, keys, vals, h, after))
            return local[-1:]

        return run

    kept, other = entering(mine, theirs, False, [attend(h) for h in range(heads)])
    attn, sums = attention_sums(queries, out_grad, local, gain, kept, other, first)
    sums = head_sum(sums)
    grad_attn, last, mine, theirs = gradient(queries, out_grad, attn, gain, sums, features)
    outs, key_parts, value_parts = [], [], []

    def differentiate(h):
        def run(after):
            normed, query, key, value = local_gradients(
                queries, keys, vals, grad_attn, attn, gain, sums, kept, other, first, features, h, tuple(outs), after
            )
            outs[:] = [normed, query]
            key_parts.append(key)
            value_parts.append(value)
            return [value]

        return run

    kept_later, other_later = entering(mine, theirs, True, [differentiate(h) for h in range(heads)])
    grad_key, grad_value = add_suffix(keys, vals, key_parts, value_parts, kept_later, other_later, last)
    normed_out, grad_query = outs
    return normed_out, grad_query, grad_key, grad_value


def solution(mesh):
    placed = (P("seq", "head"), P("seq", "head"), P("seq", "head"), P("head"), P("seq", "head"))
    return jax.shard_map(
        on_device,
        mesh=mesh,
        in_specs=placed,
        out_specs=(P("seq", "head"), P("seq", "head"), P("seq", "head"), P("seq", "head")),
        check_vma=False,
    )
```

```python
import jax
import jax.numpy as jnp
from jax import lax
from jax.experimental import pallas as pl
from jax.experimental.pallas import tpu as pltpu
from jax.sharding import PartitionSpec as P

D = 128
BLOCK = 512
HALF = 256
F32 = jnp.float32
BF16 = jnp.bfloat16
PLANES, LINE, CORES = 8, 4, 2


def dot_nn(a, b):
    return lax.dot_general(a, b, (((1,), (0,)), ((), ())), preferred_element_type=F32)


def dot_nt(a, b):
    return lax.dot_general(a, b, (((1,), (1,)), ((), ())), preferred_element_type=F32)


def dot_tn(a, b):
    return lax.dot_general(a, b, (((0,), (0,)), ((), ())), preferred_element_type=F32)


def head_cols(h):
    return slice(h * D, (h + 1) * D)


def params(mib):
    return pltpu.CompilerParams(vmem_limit_bytes=mib * 2**20)


def lower(x):
    t = lax.broadcasted_iota(jnp.int32, x.shape, 0)
    s = lax.broadcasted_iota(jnp.int32, x.shape, 1)
    return jnp.where(t >= s, x, 0.0).astype(BF16)


def upper(x):
    s = lax.broadcasted_iota(jnp.int32, x.shape, 0)
    t = lax.broadcasted_iota(jnp.int32, x.shape, 1)
    return jnp.where(t >= s, x, 0.0).astype(BF16)


TOP, BOTTOM = slice(0, HALF), slice(HALF, BLOCK)
VMEM = pl.BlockSpec(memory_space=pltpu.VMEM)
HBM = pl.BlockSpec(memory_space=pltpu.HBM)
ANY = pl.BlockSpec(memory_space=pl.ANY)


def lower_product(left, right):
    full = dot_nt(left[BOTTOM], right)
    first = lower(dot_nt(left[TOP], right[TOP]))
    return first, full[:, :HALF].astype(BF16), lower(full[:, HALF:])


def upper_product(left, right):
    full = dot_nt(left[TOP], right)
    last = upper(dot_nt(left[BOTTOM], right[BOTTOM]))
    return upper(full[:, :HALF]), full[:, HALF:].astype(BF16), last


def per_token(row):
    return jnp.transpose(jnp.broadcast_to(row, (D, row.shape[1])))


def beside(a, b):
    return jnp.concatenate([a, b], axis=1)


def block_rows(c):
    return slice(c * BLOCK, (c + 1) * BLOCK)


def places():
    me = lax.axis_index("seq")
    return me // (LINE * CORES), me // CORES % LINE, me % CORES


def shift(value, plane=0, line=0, swap=False, pair=False):
    pairs = []
    for z in range(PLANES):
        for x in range(LINE):
            for c in range(CORES):
                source = (z * LINE + x) * CORES + c
                to = x ^ 1 if pair else (x + line) % LINE
                target = ((z + plane) % PLANES * LINE + to) * CORES + (1 - c if swap else c)
                pairs.append((source, target))
    return lax.ppermute(value, "seq", pairs)


def small(body, outs, rows, name, args, after=()):
    def waiting(*refs):
        body(*refs[: len(args)], *refs[len(args) + len(after) :])

    return pl.pallas_call(
        waiting,
        in_specs=[VMEM] * len(args) + [ANY] * len(after),
        out_specs=[VMEM] * outs,
        out_shape=[jax.ShapeDtypeStruct((rows, D), F32)] * outs,
        compiler_params=params(4),
        name=name,
    )(*args, *after)


def when(condition, value):
    return jnp.where(condition, value, 0.0)


def entering(mine, theirs, reverse, beside_rounds):
    def ahead(other, me):
        return other > me if reverse else other < me

    half = mine.shape[0]
    piece = half // 2
    partner = shift(theirs, swap=True)

    def split(mine, partner, same, opposite):
        _, x, _ = places()
        for out, at in ((same, x % 2), (opposite, 1 - x % 2)):
            at = pl.ds(pl.multiple_of(at * piece, piece), piece)
            out[...] = mine[at] + partner[at]

    same, opposite = small(split, 2, piece, "split", (mine, partner))
    done = beside_rounds[0](same)
    parts = [same, shift(opposite, line=1), shift(same, line=2), shift(opposite, line=3)]

    def add(a, b, c, d, out):
        out[...] = a[...] + b[...] + c[...] + d[...]

    (plane,) = small(add, 1, piece, "add", parts, done)
    done = beside_rounds[1](plane)
    below, above = shift(plane, plane=1), shift(plane, plane=-1)

    def windows(plane, below, above, to_up, to_down):
        z, _, _ = places()
        before, after = (z + PLANES - 1) % PLANES, (z + 1) % PLANES
        up, down = (z + 2) % PLANES, (z + PLANES - 3) % PLANES
        to_up[...] = when(ahead(before, up), below[...]) + when(ahead(z, up), plane[...])
        to_down[...] = (
            when(ahead(before, down), below[...]) + when(ahead(z, down), plane[...]) + when(ahead(after, down), above[...])
        )

    to_up, to_down = small(windows, 2, piece, "windows", (plane, below, above), done)
    done = beside_rounds[2](to_up)
    from_down, from_up = shift(to_up, plane=2), shift(to_down, plane=-3)

    def spread(below, above, from_down, from_up, *refs):
        parts, outs = refs[:LINE], refs[LINE:]
        z, x, _ = places()
        before, after = (z + PLANES - 1) % PLANES, (z + 1) % PLANES
        planes = (
            when(ahead(before, z), below[...]) + when(ahead(after, z), above[...]) + from_down[...] + from_up[...]
        )
        for target, out in zip((x, x + 1 - x % 2 * 2), outs):
            total = planes
            for k, part in enumerate(parts):
                total += when(ahead((x + LINE - k) % LINE, target), part[...])
            out[...] = total

    own, sent = small(spread, 2, piece, "spread", (below, above, from_down, from_up, *parts), done)
    done = beside_rounds[3](sent)
    got = shift(sent, pair=True)

    def collect(mine, partner, own, got, kept, other):
        _, x, c = places()
        for at, part in ((x % 2, own), (1 - x % 2, got)):
            at = pl.ds(pl.multiple_of(at * piece, piece), piece)
            kept[at] = part[...] + when(ahead(1 - c, c), partner[at])
            other[at] = part[...] + when(ahead(c, 1 - c), mine[at])

    kept, other = small(collect, 2, half, "collect", (mine, partner, own, got), done)
    return kept, shift(other, swap=True)


def state_of(h, kept, other):
    _, _, c = places()
    heads = kept.shape[0] // D
    at = slice(h % heads * D, (h % heads + 1) * D)
    return jnp.where(c == h // heads, kept[at], other[at])


def products(left, right):
    length, width = left.shape
    heads = width // D
    blocks = length // BLOCK
    per_core = heads // CORES

    def body(left_hbm, right_hbm, left, right, first, mine, theirs, sems):
        copies = []
        for c in range(blocks):
            rows = pl.ds(c * BLOCK, BLOCK)
            pair = [
                pltpu.make_async_copy(left_hbm.at[rows], left.at[rows], sems.at[0, c]),
                pltpu.make_async_copy(right_hbm.at[rows], right.at[rows], sems.at[1, c]),
            ]
            for copy in pair:
                copy.start()
            copies.append(pair)
        total = [None] * heads
        for c in range(blocks):
            for copy in copies[c]:
                copy.wait()
            for h in range(heads):
                term = dot_tn(left[block_rows(c), head_cols(h)], right[block_rows(c), head_cols(h)])
                if c == 0:
                    first[head_cols(h)] = term
                total[h] = term if c == 0 else total[h] + term
        _, _, core = places()
        for h in range(heads):
            store_half(core, h, per_core, total[h], mine, theirs)

    half_shape = jax.ShapeDtypeStruct((width // CORES, D), F32)
    return pl.pallas_call(
        body,
        in_specs=[HBM, HBM],
        out_specs=[VMEM] * 5,
        out_shape=[
            jax.ShapeDtypeStruct(left.shape, BF16),
            jax.ShapeDtypeStruct(right.shape, BF16),
            jax.ShapeDtypeStruct((width, D), F32),
            half_shape,
            half_shape,
        ],
        scratch_shapes=[pltpu.SemaphoreType.DMA((2, blocks))],
        compiler_params=params(12),
        name="products",
    )(pltpu.with_memory_space_constraint(left, pltpu.HBM), pltpu.with_memory_space_constraint(right, pltpu.HBM))


def store_half(core, h, per_core, value, mine, theirs):
    at = head_cols(h % per_core)

    @pl.when(core == h // per_core)
    def _():
        mine[at] = value

    @pl.when(core != h // per_core)
    def _():
        theirs[at] = value


def local_attention(q, k, v, h, after):
    length = q.shape[0]

    def body(q, k, v, _, out):
        for c in range(length // BLOCK):
            rows = block_rows(c)
            qv, kv, vv = (x[rows, head_cols(h)] for x in (q, k, v))
            a, b, d = lower_product(qv, kv)
            out[c * BLOCK : c * BLOCK + HALF] = dot_nn(a, vv[TOP])
            out[c * BLOCK + HALF : (c + 1) * BLOCK] = dot_nn(beside(b, d), vv)

    return pl.pallas_call(
        body,
        in_specs=[VMEM, VMEM, VMEM, ANY],
        out_specs=VMEM,
        out_shape=jax.ShapeDtypeStruct((length, D), F32),
        compiler_params=params(12),
        cost_estimate=pl.CostEstimate(
            flops=length // BLOCK * 4 * BLOCK * BLOCK * D, bytes_accessed=length * D * 10, transcendentals=0
        ),
        name="local_attention",
    )(q, k, v, after)


def attention_sums(q, grad, local, gain, kept, other, first):
    length, width = q.shape
    heads = width // D

    def body(q, grad, *refs):
        local, (gain, kept, other, first, attn, sums) = refs[:heads], refs[heads:]
        for c in range(length // BLOCK):
            rows = block_rows(c)
            square = jnp.zeros((BLOCK, D), F32)
            inner = jnp.zeros((BLOCK, D), F32)
            for h in range(heads):
                cols = head_cols(h)
                prefix = state_of(h, kept, other)
                if c > 0:
                    prefix += first[cols]
                a = local[h][rows] + dot_nn(q[rows, cols], prefix.astype(BF16))
                attn[rows, cols] = a
                square += a * a
                inner += a * (gain[:, cols] * grad[rows, cols].astype(F32))
            sums[0:1, rows] = jnp.sum(jnp.transpose(square), axis=0, keepdims=True)
            sums[1:2, rows] = jnp.sum(jnp.transpose(inner), axis=0, keepdims=True)

    return pl.pallas_call(
        body,
        in_specs=[VMEM] * (6 + heads),
        out_specs=[VMEM] * 2,
        out_shape=[
            jax.ShapeDtypeStruct((length, width), F32),
            jax.ShapeDtypeStruct((2, length), F32),
        ],
        compiler_params=params(16),
        name="attention_sums",
    )(q, grad, *local, gain, kept, other, first)


def gradient(q, grad, attn, gain, sums, features):
    length, width = q.shape
    heads = width // D
    blocks = length // BLOCK

    def body(q, grad, attn, gain, sums, out, last, mine, theirs):
        total = [None] * heads
        for c in range(blocks):
            rows = block_rows(c)
            root = jnp.sqrt(sums[0:1, rows] / features + 1e-05)
            inverse = per_token(1.0 / root)
            weight = per_token(sums[1:2, rows] / (features * root**3))
            for h in range(heads):
                cols = head_cols(h)
                scaled = gain[:, cols] * grad[rows, cols].astype(F32)
                g = (scaled * inverse - attn[rows, cols] * weight).astype(BF16)
                out[rows, cols] = g
                term = dot_tn(q[rows, cols], g)
                total[h] = term if c == 0 else total[h] + term
                if c == blocks - 1:
                    last[cols] = term
        _, _, core = places()
        for h in range(heads):
            store_half(core, h, heads // CORES, total[h], mine, theirs)

    half_shape = jax.ShapeDtypeStruct((width // CORES, D), F32)
    return pl.pallas_call(
        body,
        in_specs=[VMEM] * 5,
        out_specs=[VMEM] * 4,
        out_shape=[
            jax.ShapeDtypeStruct((length, width), BF16),
            jax.ShapeDtypeStruct((width, D), F32),
            half_shape,
            half_shape,
        ],
        compiler_params=params(16),
        name="gradient",
    )(q, grad, attn, gain, sums)


def local_gradients(q, k, v, g, attn, gain, sums, kept, other, first, features, h, outs, after):
    length, width = q.shape
    blocks = length // BLOCK
    cols = head_cols(h)

    def body(q, k, v, g, attn, gain, sums, kept, other, first, *refs):
        normed, dq, dk, dv, normed_here, dq_here, sems = refs[len(outs) + 1 :]
        copies = []

        def send(here, out, i, c):
            copy = pltpu.make_async_copy(here.at[block_rows(c)], out.at[block_rows(c), cols], sems.at[i, c])
            copy.start()
            copies.append(copy)

        state = state_of(h, kept, other)
        for c in range(blocks):
            rows = block_rows(c)
            root = jnp.sqrt(sums[0:1, rows] / features + 1e-05)
            normed_here[rows] = (gain[:, cols] * (attn[rows, cols] * per_token(1.0 / root))).astype(BF16)
            send(normed_here, normed, 0, c)
            qv, kv, vv, gv = (x[rows, cols] for x in (q, k, v, g))
            prefix = state + first[cols] if c > 0 else state
            carried = dot_nt(gv, prefix.astype(BF16))
            a, b, d = lower_product(gv, vv)
            top, bottom = slice(c * BLOCK, c * BLOCK + HALF), slice(c * BLOCK + HALF, (c + 1) * BLOCK)
            dq_here[top] = (dot_nn(a, kv[TOP]) + carried[TOP]).astype(BF16)
            dq_here[bottom] = (dot_nn(beside(b, d), kv) + carried[BOTTOM]).astype(BF16)
            send(dq_here, dq, 1, c)
            a, b, d = upper_product(vv, gv)
            dk[top] = dot_nn(beside(a, b), qv)
            dk[bottom] = dot_nn(d, qv[BOTTOM])
            a, b, d = upper_product(kv, qv)
            dv[top] = dot_nn(beside(a, b), gv)
            dv[bottom] = dot_nn(d, gv[BOTTOM])
        for copy in copies:
            copy.wait()

    return pl.pallas_call(
        body,
        in_specs=[VMEM] * 10 + [HBM] * len(outs) + [ANY],
        out_specs=[HBM, HBM, VMEM, VMEM],
        out_shape=[jax.ShapeDtypeStruct((length, width), BF16)] * 2 + [jax.ShapeDtypeStruct((length, D), F32)] * 2,
        scratch_shapes=[pltpu.VMEM((length, D), BF16)] * 2 + [pltpu.SemaphoreType.DMA((2, blocks))],
        input_output_aliases={10 + i: i for i in range(len(outs))},
        compiler_params=params(20),
        cost_estimate=pl.CostEstimate(
            flops=blocks * 12 * BLOCK * BLOCK * D, bytes_accessed=length * D * 20, transcendentals=0
        ),
        name="local_gradients",
    )(q, k, v, g, attn, gain, sums, kept, other, first, *outs, after)


def add_suffix(k, v, dk, dv, kept, other, last):
    length, width = k.shape
    heads = width // D
    steps = length // HALF

    def body(k, v, *refs):
        dk, dv = refs[:heads], refs[heads : 2 * heads]
        kept, other, last, out_k, out_v, here_k, here_v, sems = refs[2 * heads :]
        copies = []
        for i in range(steps):
            rows = slice(i * HALF, (i + 1) * HALF)
            for h in range(heads):
                cols = head_cols(h)
                suffix = state_of(h, kept, other)
                if (i + 1) * HALF <= length - BLOCK:
                    suffix += last[cols]
                suffix = suffix.astype(BF16)
                here_k[rows, cols] = (dk[h][rows] + dot_nt(v[rows, cols], suffix)).astype(BF16)
                here_v[rows, cols] = (dv[h][rows] + dot_nn(k[rows, cols], suffix)).astype(BF16)
            for here, out, j in ((here_k, out_k, 0), (here_v, out_v, 1)):
                copy = pltpu.make_async_copy(here.at[rows], out.at[rows], sems.at[j, i])
                copy.start()
                copies.append(copy)
        for copy in copies:
            copy.wait()

    shape = jax.ShapeDtypeStruct((length, width), BF16)
    return pl.pallas_call(
        body,
        in_specs=[VMEM] * (5 + 2 * heads),
        out_specs=[HBM, HBM],
        out_shape=[shape, shape],
        scratch_shapes=[pltpu.VMEM((length, width), BF16)] * 2 + [pltpu.SemaphoreType.DMA((2, steps))],
        compiler_params=params(16),
        name="add_suffix",
    )(k, v, *dk, *dv, kept, other, last)


def head_sum(part):
    count = lax.axis_size("head")
    total = part
    for k in range(1, count):
        total = total + lax.ppermute(part, "head", [(i, (i + k) % count) for i in range(count)])
    return total


def on_device(queries, token_keys, values, norm_gain, out_grad):
    heads = queries.shape[1] // D
    features = lax.axis_size("head") * heads * D
    gain = norm_gain.reshape(1, heads * D)
    keys, vals, first, mine, theirs = products(token_keys, values)
    local = []

    def attend(h):
        def run(after):
            local.append(local_attention(queries, keys, vals, h, after))
            return local[-1:]

        return run

    kept, other = entering(mine, theirs, False, [attend(h) for h in range(heads)])
    attn, sums = attention_sums(queries, out_grad, local, gain, kept, other, first)
    sums = head_sum(sums)
    grad_attn, last, mine, theirs = gradient(queries, out_grad, attn, gain, sums, features)
    outs, key_parts, value_parts = [], [], []

    def differentiate(h):
        def run(after):
            normed, query, key, value = local_gradients(
                queries, keys, vals, grad_attn, attn, gain, sums, kept, other, first, features, h, tuple(outs), after
            )
            outs[:] = [normed, query]
            key_parts.append(key)
            value_parts.append(value)
            return [value]

        return run

    kept_later, other_later = entering(mine, theirs, True, [differentiate(h) for h in range(heads)])
    grad_key, grad_value = add_suffix(keys, vals, key_parts, value_parts, kept_later, other_later, last)
    normed_out, grad_query = outs
    return normed_out, grad_query, grad_key, grad_value


def solution(mesh):
    placed = (P("seq", "head"), P("seq", "head"), P("seq", "head"), P("head"), P("seq", "head"))
    return jax.shard_map(
        on_device,
        mesh=mesh,
        in_specs=placed,
        out_specs=(P("seq", "head"), P("seq", "head"), P("seq", "head"), P("seq", "head")),
        check_vma=False,
    )
```

```python
import jax
import jax.numpy as jnp
from jax import lax
from jax.experimental import pallas as pl
from jax.experimental.pallas import tpu as pltpu
from jax.sharding import PartitionSpec as P

D = 128
BLOCK = 512
HALF = 256
F32 = jnp.float32
BF16 = jnp.bfloat16
PLANES, LINE, CORES = 8, 4, 2


def dot_nn(a, b):
    return lax.dot_general(a, b, (((1,), (0,)), ((), ())), preferred_element_type=F32)


def dot_nt(a, b):
    return lax.dot_general(a, b, (((1,), (1,)), ((), ())), preferred_element_type=F32)


def dot_tn(a, b):
    return lax.dot_general(a, b, (((0,), (0,)), ((), ())), preferred_element_type=F32)


def head_cols(h):
    return slice(h * D, (h + 1) * D)


def params(mib):
    return pltpu.CompilerParams(vmem_limit_bytes=mib * 2**20)


def lower(x):
    t = lax.broadcasted_iota(jnp.int32, x.shape, 0)
    s = lax.broadcasted_iota(jnp.int32, x.shape, 1)
    return jnp.where(t >= s, x, 0.0).astype(BF16)


def upper(x):
    s = lax.broadcasted_iota(jnp.int32, x.shape, 0)
    t = lax.broadcasted_iota(jnp.int32, x.shape, 1)
    return jnp.where(t >= s, x, 0.0).astype(BF16)


TOP, BOTTOM = slice(0, HALF), slice(HALF, BLOCK)
VMEM = pl.BlockSpec(memory_space=pltpu.VMEM)
HBM = pl.BlockSpec(memory_space=pltpu.HBM)
ANY = pl.BlockSpec(memory_space=pl.ANY)


def lower_product(left, right):
    full = dot_nt(left[BOTTOM], right)
    first = lower(dot_nt(left[TOP], right[TOP]))
    return first, full[:, :HALF].astype(BF16), lower(full[:, HALF:])


def upper_product(left, right):
    full = dot_nt(left[TOP], right)
    last = upper(dot_nt(left[BOTTOM], right[BOTTOM]))
    return upper(full[:, :HALF]), full[:, HALF:].astype(BF16), last


def per_token(row):
    return jnp.transpose(jnp.broadcast_to(row, (D, row.shape[1])))


def beside(a, b):
    return jnp.concatenate([a, b], axis=1)


def block_rows(c):
    return slice(c * BLOCK, (c + 1) * BLOCK)


def places():
    me = lax.axis_index("seq")
    return me // (LINE * CORES), me // CORES % LINE, me % CORES


def shift(value, plane=0, line=0, swap=False, pair=False):
    pairs = []
    for z in range(PLANES):
        for x in range(LINE):
            for c in range(CORES):
                source = (z * LINE + x) * CORES + c
                to = x ^ 1 if pair else (x + line) % LINE
                target = ((z + plane) % PLANES * LINE + to) * CORES + (1 - c if swap else c)
                pairs.append((source, target))
    return lax.ppermute(value, "seq", pairs)


def small(body, outs, rows, name, args, after=()):
    def waiting(*refs):
        body(*refs[: len(args)], *refs[len(args) + len(after) :])

    return pl.pallas_call(
        waiting,
        in_specs=[VMEM] * len(args) + [ANY] * len(after),
        out_specs=[VMEM] * outs,
        out_shape=[jax.ShapeDtypeStruct((rows, D), F32)] * outs,
        compiler_params=params(4),
        name=name,
    )(*args, *after)


def when(condition, value):
    return jnp.where(condition, value, 0.0)


def entering(mine, theirs, reverse, beside_rounds):
    def ahead(other, me):
        return other > me if reverse else other < me

    half = mine.shape[0]
    piece = half // 2
    partner = shift(theirs, swap=True)

    def split(mine, partner, same, opposite):
        _, x, _ = places()
        for out, at in ((same, x % 2), (opposite, 1 - x % 2)):
            at = pl.ds(pl.multiple_of(at * piece, piece), piece)
            out[...] = mine[at] + partner[at]

    same, opposite = small(split, 2, piece, "split", (mine, partner))
    done = beside_rounds[0](same)
    parts = [same, shift(opposite, line=1), shift(same, line=2), shift(opposite, line=3)]

    def add(a, b, c, d, out):
        out[...] = a[...] + b[...] + c[...] + d[...]

    (plane,) = small(add, 1, piece, "add", parts, done)
    done = beside_rounds[1](plane)
    below, above = shift(plane, plane=1), shift(plane, plane=-1)

    def windows(plane, below, above, to_up, to_down):
        z, _, _ = places()
        before, after = (z + PLANES - 1) % PLANES, (z + 1) % PLANES
        up, down = (z + 2) % PLANES, (z + PLANES - 3) % PLANES
        to_up[...] = when(ahead(before, up), below[...]) + when(ahead(z, up), plane[...])
        to_down[...] = (
            when(ahead(before, down), below[...]) + when(ahead(z, down), plane[...]) + when(ahead(after, down), above[...])
        )

    to_up, to_down = small(windows, 2, piece, "windows", (plane, below, above), done)
    done = beside_rounds[2](to_up)
    from_down, from_up = shift(to_up, plane=2), shift(to_down, plane=-3)

    def spread(below, above, from_down, from_up, *refs):
        parts, outs = refs[:LINE], refs[LINE:]
        z, x, _ = places()
        before, after = (z + PLANES - 1) % PLANES, (z + 1) % PLANES
        planes = (
            when(ahead(before, z), below[...]) + when(ahead(after, z), above[...]) + from_down[...] + from_up[...]
        )
        for target, out in zip((x, x + 1 - x % 2 * 2), outs):
            total = planes
            for k, part in enumerate(parts):
                total += when(ahead((x + LINE - k) % LINE, target), part[...])
            out[...] = total

    own, sent = small(spread, 2, piece, "spread", (below, above, from_down, from_up, *parts), done)
    done = beside_rounds[3](sent)
    got = shift(sent, pair=True)

    def collect(mine, partner, own, got, kept, other):
        _, x, c = places()
        for at, part in ((x % 2, own), (1 - x % 2, got)):
            at = pl.ds(pl.multiple_of(at * piece, piece), piece)
            kept[at] = part[...] + when(ahead(1 - c, c), partner[at])
            other[at] = part[...] + when(ahead(c, 1 - c), mine[at])

    kept, other = small(collect, 2, half, "collect", (mine, partner, own, got), done)
    return kept, shift(other, swap=True)


def columns(is_mine, i, per_core):
    _, _, c = places()
    half = c if is_mine else 1 - c
    return pl.ds(pl.multiple_of((half * per_core + i) * D, D), D)


def bring(left, right):
    length, width = left.shape
    per_core = width // D // CORES

    def body(left_hbm, right_hbm, left, right, first, total, sems):
        _, _, c = places()
        copies = []
        for i, half in enumerate((1 - c, c)):
            cols = pl.ds(pl.multiple_of(half * per_core * D, per_core * D), per_core * D)
            for j, (source, target) in enumerate(((left_hbm, left), (right_hbm, right))):
                copy = pltpu.make_async_copy(source.at[:, cols], target.at[:, cols], sems.at[i, j])
                copy.start()
                copies.append(copy)
        copies[0].wait()
        copies[1].wait()
        multiply(left, right, False, per_core, first, total)
        copies[2].wait()
        copies[3].wait()

    state = jax.ShapeDtypeStruct((width // CORES, D), F32)
    return pl.pallas_call(
        body,
        in_specs=[HBM, HBM],
        out_specs=[VMEM] * 4,
        out_shape=[jax.ShapeDtypeStruct(left.shape, BF16), jax.ShapeDtypeStruct(right.shape, BF16), state, state],
        scratch_shapes=[pltpu.SemaphoreType.DMA((CORES, 2))],
        compiler_params=params(12),
        name="bring",
    )(pltpu.with_memory_space_constraint(left, pltpu.HBM), pltpu.with_memory_space_constraint(right, pltpu.HBM))


def multiply(left, right, is_mine, per_core, first, total):
    for i in range(per_core):
        cols = columns(is_mine, i, per_core)
        one = dot_tn(left[:BLOCK, cols], right[:BLOCK, cols])
        first[head_cols(i)] = one
        total[head_cols(i)] = one + dot_tn(left[BLOCK:, cols], right[BLOCK:, cols])


def products(left, right):
    width = left.shape[1]

    def body(left, right, first, total):
        multiply(left, right, True, width // D // CORES, first, total)

    state = jax.ShapeDtypeStruct((width // CORES, D), F32)
    return pl.pallas_call(
        body,
        in_specs=[VMEM] * 2,
        out_specs=[VMEM] * 2,
        out_shape=[state, state],
        compiler_params=params(12),
        name="products",
    )(left, right)


def local_attention(q, k, v, is_mine, i, after):
    length, width = q.shape

    def body(q, k, v, _, out):
        cols = columns(is_mine, i, width // D // CORES)
        for c in range(length // BLOCK):
            rows = block_rows(c)
            qv, kv, vv = (x[rows, cols] for x in (q, k, v))
            a, b, d = lower_product(qv, kv)
            out[c * BLOCK : c * BLOCK + HALF] = dot_nn(a, vv[TOP])
            out[c * BLOCK + HALF : (c + 1) * BLOCK] = dot_nn(beside(b, d), vv)

    return pl.pallas_call(
        body,
        in_specs=[VMEM, VMEM, VMEM, ANY],
        out_specs=VMEM,
        out_shape=jax.ShapeDtypeStruct((length, D), F32),
        compiler_params=params(12),
        cost_estimate=pl.CostEstimate(
            flops=length // BLOCK * 4 * BLOCK * BLOCK * D, bytes_accessed=length * D * 10, transcendentals=0
        ),
        name="local_attention",
    )(q, k, v, after)


def attention_sums(q, grad, local, gain, state, first, is_mine, sums):
    length = q.shape[0]
    per_core = len(local)

    def body(q, grad, *refs):
        local, (gain, state, first, *before, attn, sums) = refs[:per_core], refs[per_core:]
        for c in range(length // BLOCK):
            rows = block_rows(c)
            square = jnp.zeros((BLOCK, D), F32)
            inner = jnp.zeros((BLOCK, D), F32)
            for i in range(per_core):
                cols = columns(is_mine, i, per_core)
                prefix = state[head_cols(i)]
                if c > 0:
                    prefix += first[head_cols(i)]
                a = local[i][rows] + dot_nn(q[rows, cols], prefix.astype(BF16))
                attn[rows, head_cols(i)] = a
                square += a * a
                inner += a * (gain[:, cols] * grad[rows, cols].astype(F32))
            for j, part in enumerate((square, inner)):
                row = jnp.sum(jnp.transpose(part), axis=0, keepdims=True)
                sums[j : j + 1, rows] = row + before[0][j : j + 1, rows] if before else row

    return pl.pallas_call(
        body,
        in_specs=[VMEM] * (5 + per_core + len(sums)),
        out_specs=[VMEM] * 2,
        out_shape=[
            jax.ShapeDtypeStruct((length, per_core * D), F32),
            jax.ShapeDtypeStruct((2, length), F32),
        ],
        compiler_params=params(16),
        name="attention_sums",
    )(q, grad, *local, gain, state, first, *sums)


def gradient(q, grad, attn, gain, sums, features, is_mine):
    length, width = attn.shape
    per_core = width // D
    blocks = length // BLOCK

    def body(q, grad, attn, gain, sums, out, last, total):
        for c in range(blocks):
            rows = block_rows(c)
            root = jnp.sqrt(sums[0:1, rows] / features + 1e-05)
            inverse = per_token(1.0 / root)
            weight = per_token(sums[1:2, rows] / (features * root**3))
            for i in range(per_core):
                cols = columns(is_mine, i, per_core)
                scaled = gain[:, cols] * grad[rows, cols].astype(F32)
                g = (scaled * inverse - attn[rows, head_cols(i)] * weight).astype(BF16)
                out[rows, head_cols(i)] = g
                term = dot_tn(q[rows, cols], g)
                total[head_cols(i)] = term if c == 0 else total[head_cols(i)] + term
                if c == blocks - 1:
                    last[head_cols(i)] = term

    state = jax.ShapeDtypeStruct((width, D), F32)
    return pl.pallas_call(
        body,
        in_specs=[VMEM] * 5,
        out_specs=[VMEM] * 3,
        out_shape=[jax.ShapeDtypeStruct((length, width), BF16), state, state],
        compiler_params=params(16),
        name="gradient",
    )(q, grad, attn, gain, sums)


def local_gradients(q, k, v, g, attn, gain, sums, state, first, features, is_mine, i, outs, after):
    length, width = q.shape
    blocks = length // BLOCK
    here = head_cols(i)

    def body(q, k, v, g, attn, gain, sums, state, first, *refs):
        normed, dq, dk, dv, normed_here, dq_here, sems = refs[len(outs) + 1 :]
        cols = columns(is_mine, i, width // D // CORES)
        copies = []

        def send(source, out, j, c):
            copy = pltpu.make_async_copy(source.at[block_rows(c)], out.at[block_rows(c), cols], sems.at[j, c])
            copy.start()
            copies.append(copy)

        for c in range(blocks):
            rows = block_rows(c)
            root = jnp.sqrt(sums[0:1, rows] / features + 1e-05)
            normed_here[rows] = (gain[:, cols] * (attn[rows, here] * per_token(1.0 / root))).astype(BF16)
            send(normed_here, normed, 0, c)
            qv, kv, vv, gv = q[rows, cols], k[rows, cols], v[rows, cols], g[rows, here]
            prefix = state[here] + first[here] if c > 0 else state[here]
            carried = dot_nt(gv, prefix.astype(BF16))
            a, b, d = lower_product(gv, vv)
            top, bottom = slice(c * BLOCK, c * BLOCK + HALF), slice(c * BLOCK + HALF, (c + 1) * BLOCK)
            dq_here[top] = (dot_nn(a, kv[TOP]) + carried[TOP]).astype(BF16)
            dq_here[bottom] = (dot_nn(beside(b, d), kv) + carried[BOTTOM]).astype(BF16)
            send(dq_here, dq, 1, c)
            a, b, d = upper_product(vv, gv)
            dk[top] = dot_nn(beside(a, b), qv)
            dk[bottom] = dot_nn(d, qv[BOTTOM])
            a, b, d = upper_product(kv, qv)
            dv[top] = dot_nn(beside(a, b), gv)
            dv[bottom] = dot_nn(d, gv[BOTTOM])
        for copy in copies:
            copy.wait()

    return pl.pallas_call(
        body,
        in_specs=[VMEM] * 9 + [HBM] * len(outs) + [ANY],
        out_specs=[HBM, HBM, VMEM, VMEM],
        out_shape=[jax.ShapeDtypeStruct((length, width), BF16)] * 2 + [jax.ShapeDtypeStruct((length, D), F32)] * 2,
        scratch_shapes=[pltpu.VMEM((length, D), BF16)] * 2 + [pltpu.SemaphoreType.DMA((2, blocks))],
        input_output_aliases={9 + j: j for j in range(len(outs))},
        compiler_params=params(20),
        cost_estimate=pl.CostEstimate(
            flops=blocks * 12 * BLOCK * BLOCK * D, bytes_accessed=length * D * 20, transcendentals=0
        ),
        name="local_gradients",
    )(q, k, v, g, attn, gain, sums, state, first, *outs, after)


def add_suffix(k, v, dk, dv, state, last, is_mine, outs):
    length, width = k.shape
    per_core = len(dk)
    steps = 2
    part = length // steps

    def body(k, v, *refs):
        dk, dv = refs[:per_core], refs[per_core : 2 * per_core]
        state, last = refs[2 * per_core : 2 * per_core + 2]
        out_k, out_v, here_k, here_v, sems = refs[2 * per_core + 2 + len(outs) :]
        _, _, c = places()
        half = c if is_mine else 1 - c
        target = pl.ds(pl.multiple_of(half * per_core * D, per_core * D), per_core * D)
        copies = []
        for step in range(steps):
            rows = slice(step * part, (step + 1) * part)
            for i in range(per_core):
                cols, here = columns(is_mine, i, per_core), head_cols(i)
                suffix = state[here]
                if step * part < length - BLOCK:
                    suffix += last[here]
                suffix = suffix.astype(BF16)
                here_k[rows, here] = (dk[i][rows] + dot_nt(v[rows, cols], suffix)).astype(BF16)
                here_v[rows, here] = (dv[i][rows] + dot_nn(k[rows, cols], suffix)).astype(BF16)
            for j, (source, out) in enumerate(((here_k, out_k), (here_v, out_v))):
                copy = pltpu.make_async_copy(source.at[rows], out.at[rows, target], sems.at[j, step])
                copy.start()
                copies.append(copy)
        for copy in copies:
            copy.wait()

    shape = jax.ShapeDtypeStruct((length, width), BF16)
    inputs = 4 + 2 * per_core
    return pl.pallas_call(
        body,
        in_specs=[VMEM] * inputs + [HBM] * len(outs),
        out_specs=[HBM, HBM],
        out_shape=[shape, shape],
        scratch_shapes=[pltpu.VMEM((length, per_core * D), BF16)] * 2 + [pltpu.SemaphoreType.DMA((2, steps))],
        input_output_aliases={inputs + j: j for j in range(len(outs))},
        compiler_params=params(16),
        name="add_suffix",
    )(k, v, *dk, *dv, state, last, *outs)


def head_sum(part):
    count = lax.axis_size("head")
    total = part
    for k in range(1, count):
        total = total + lax.ppermute(part, "head", [(i, (i + k) % count) for i in range(count)])
    return total


def on_device(queries, token_keys, values, norm_gain, out_grad):
    heads = queries.shape[1] // D
    features = lax.axis_size("head") * heads * D
    gain = norm_gain.reshape(1, heads * D)
    per_core = heads // CORES
    order = [(is_mine, i) for is_mine in (True, False) for i in range(per_core)]
    keys, vals, first_theirs, theirs = bring(token_keys, values)
    first_mine, mine = products(keys, vals)
    first = {True: first_mine, False: first_theirs}
    local = {True: [], False: []}

    def attend(is_mine, i):
        def run(after):
            local[is_mine].append(local_attention(queries, keys, vals, is_mine, i, after))
            return local[is_mine][-1:]

        return run

    kept, other = entering(mine, theirs, False, [attend(*head) for head in order])
    before = {True: kept, False: other}
    attn, sums = {}, ()
    for is_mine in (True, False):
        attn[is_mine], part = attention_sums(
            queries, out_grad, local[is_mine], gain, before[is_mine], first[is_mine], is_mine, sums
        )
        sums = (part,)
    sums = head_sum(part)
    grad_attn, last, total = {}, {}, {}
    for is_mine in (False, True):
        grad_attn[is_mine], last[is_mine], total[is_mine] = gradient(
            queries, out_grad, attn[is_mine], gain, sums, features, is_mine
        )
    outs, key_parts, value_parts = [], {True: [], False: []}, {True: [], False: []}

    def differentiate(is_mine, i):
        def run(after):
            normed, query, key, value = local_gradients(
                queries,
                keys,
                vals,
                grad_attn[is_mine],
                attn[is_mine],
                gain,
                sums,
                before[is_mine],
                first[is_mine],
                features,
                is_mine,
                i,
                tuple(outs),
                after,
            )
            outs[:] = [normed, query]
            key_parts[is_mine].append(key)
            value_parts[is_mine].append(value)
            return [value]

        return run

    kept, other = entering(total[True], total[False], True, [differentiate(*head) for head in order])
    normed_out, grad_query = outs
    outs = ()
    for is_mine, state in ((True, kept), (False, other)):
        outs = add_suffix(keys, vals, key_parts[is_mine], value_parts[is_mine], state, last[is_mine], is_mine, outs)
    grad_key, grad_value = outs
    return normed_out, grad_query, grad_key, grad_value


def solution(mesh):
    placed = (P("seq", "head"), P("seq", "head"), P("seq", "head"), P("head"), P("seq", "head"))
    return jax.shard_map(
        on_device,
        mesh=mesh,
        in_specs=placed,
        out_specs=(P("seq", "head"), P("seq", "head"), P("seq", "head"), P("seq", "head")),
        check_vma=False,
    )
```

```python
import jax
import jax.numpy as jnp
from jax import lax
from jax.experimental import pallas as pl
from jax.experimental.pallas import tpu as pltpu
from jax.sharding import PartitionSpec as P

D = 128
BLOCK = 512
HALF = 256
F32 = jnp.float32
BF16 = jnp.bfloat16
PLANES, LINE, CORES = 8, 4, 2


def dot_nn(a, b):
    return lax.dot_general(a, b, (((1,), (0,)), ((), ())), preferred_element_type=F32)


def dot_nt(a, b):
    return lax.dot_general(a, b, (((1,), (1,)), ((), ())), preferred_element_type=F32)


def dot_tn(a, b):
    return lax.dot_general(a, b, (((0,), (0,)), ((), ())), preferred_element_type=F32)


def head_cols(h):
    return slice(h * D, (h + 1) * D)


def params(mib):
    return pltpu.CompilerParams(vmem_limit_bytes=mib * 2**20)


def lower(x):
    t = lax.broadcasted_iota(jnp.int32, x.shape, 0)
    s = lax.broadcasted_iota(jnp.int32, x.shape, 1)
    return jnp.where(t >= s, x, 0.0).astype(BF16)


def upper(x):
    s = lax.broadcasted_iota(jnp.int32, x.shape, 0)
    t = lax.broadcasted_iota(jnp.int32, x.shape, 1)
    return jnp.where(t >= s, x, 0.0).astype(BF16)


TOP, BOTTOM = slice(0, HALF), slice(HALF, BLOCK)
VMEM = pl.BlockSpec(memory_space=pltpu.VMEM)
HBM = pl.BlockSpec(memory_space=pltpu.HBM)
ANY = pl.BlockSpec(memory_space=pl.ANY)


def lower_product(left, right):
    full = dot_nt(left[BOTTOM], right)
    first = lower(dot_nt(left[TOP], right[TOP]))
    return first, full[:, :HALF].astype(BF16), lower(full[:, HALF:])


def upper_product(left, right):
    full = dot_nt(left[TOP], right)
    last = upper(dot_nt(left[BOTTOM], right[BOTTOM]))
    return upper(full[:, :HALF]), full[:, HALF:].astype(BF16), last


def per_token(row):
    return jnp.transpose(jnp.broadcast_to(row, (D, row.shape[1])))


def beside(a, b):
    return jnp.concatenate([a, b], axis=1)


def block_rows(c):
    return slice(c * BLOCK, (c + 1) * BLOCK)


def places():
    me = lax.axis_index("seq")
    return me // (LINE * CORES), me // CORES % LINE, me % CORES


def shift(value, plane=0, line=0, swap=False, pair=False):
    pairs = []
    for z in range(PLANES):
        for x in range(LINE):
            for c in range(CORES):
                source = (z * LINE + x) * CORES + c
                to = x ^ 1 if pair else (x + line) % LINE
                target = ((z + plane) % PLANES * LINE + to) * CORES + (1 - c if swap else c)
                pairs.append((source, target))
    return lax.ppermute(value, "seq", pairs)


def small(body, outs, rows, name, args, after=()):
    def waiting(*refs):
        body(*refs[: len(args)], *refs[len(args) + len(after) :])

    return pl.pallas_call(
        waiting,
        in_specs=[VMEM] * len(args) + [ANY] * len(after),
        out_specs=[VMEM] * outs,
        out_shape=[jax.ShapeDtypeStruct((rows, D), F32)] * outs,
        compiler_params=params(4),
        name=name,
    )(*args, *after)


def when(condition, value):
    return jnp.where(condition, value, 0.0)


def entering(mine, theirs, reverse, beside_rounds):
    def ahead(other, me):
        return other > me if reverse else other < me

    half = mine.shape[0]
    piece = half // 2
    partner = shift(theirs, swap=True)

    def split(mine, partner, same, opposite):
        _, x, _ = places()
        for out, at in ((same, x % 2), (opposite, 1 - x % 2)):
            at = pl.ds(pl.multiple_of(at * piece, piece), piece)
            out[...] = mine[at] + partner[at]

    same, opposite = small(split, 2, piece, "split", (mine, partner))
    done = beside_rounds[0](same)
    parts = [same, shift(opposite, line=1), shift(same, line=2), shift(opposite, line=3)]

    def add(a, b, c, d, out):
        out[...] = a[...] + b[...] + c[...] + d[...]

    (plane,) = small(add, 1, piece, "add", parts, done)
    done = beside_rounds[1](plane)
    below, above = shift(plane, plane=1), shift(plane, plane=-1)

    def windows(plane, below, above, to_up, to_down):
        z, _, _ = places()
        before, after = (z + PLANES - 1) % PLANES, (z + 1) % PLANES
        up, down = (z + 2) % PLANES, (z + PLANES - 3) % PLANES
        to_up[...] = when(ahead(before, up), below[...]) + when(ahead(z, up), plane[...])
        to_down[...] = (
            when(ahead(before, down), below[...]) + when(ahead(z, down), plane[...]) + when(ahead(after, down), above[...])
        )

    to_up, to_down = small(windows, 2, piece, "windows", (plane, below, above), done)
    done = beside_rounds[2](to_up)
    from_down, from_up = shift(to_up, plane=2), shift(to_down, plane=-3)

    def spread(below, above, from_down, from_up, *refs):
        parts, outs = refs[:LINE], refs[LINE:]
        z, x, _ = places()
        before, after = (z + PLANES - 1) % PLANES, (z + 1) % PLANES
        planes = (
            when(ahead(before, z), below[...]) + when(ahead(after, z), above[...]) + from_down[...] + from_up[...]
        )
        for target, out in zip((x, x + 1 - x % 2 * 2), outs):
            total = planes
            for k, part in enumerate(parts):
                total += when(ahead((x + LINE - k) % LINE, target), part[...])
            out[...] = total

    own, sent = small(spread, 2, piece, "spread", (below, above, from_down, from_up, *parts), done)
    done = beside_rounds[3](sent)
    got = shift(sent, pair=True)

    def collect(mine, partner, own, got, kept, other):
        _, x, c = places()
        for at, part in ((x % 2, own), (1 - x % 2, got)):
            at = pl.ds(pl.multiple_of(at * piece, piece), piece)
            kept[at] = part[...] + when(ahead(1 - c, c), partner[at])
            other[at] = part[...] + when(ahead(c, 1 - c), mine[at])

    kept, other = small(collect, 2, half, "collect", (mine, partner, own, got), done)
    return kept, shift(other, swap=True)


def columns(is_mine, i, per_core):
    _, _, c = places()
    half = c if is_mine else 1 - c
    return pl.ds(pl.multiple_of((half * per_core + i) * D, D), D)


def bring(left, right):
    length, width = left.shape
    per_core = width // D // CORES

    def body(left_hbm, right_hbm, left, right, first, total, sems):
        _, _, c = places()
        copies = []
        for i, half in enumerate((1 - c, c)):
            cols = pl.ds(pl.multiple_of(half * per_core * D, per_core * D), per_core * D)
            for b in range(length // BLOCK):
                at = (pl.ds(b * BLOCK, BLOCK), cols)
                pair = []
                for j, (source, target) in enumerate(((left_hbm, left), (right_hbm, right))):
                    pair.append(pltpu.make_async_copy(source.at[at], target.at[at], sems.at[i, b, j]))
                    pair[-1].start()
                copies.append(pair)
        for b, pair in enumerate(copies):
            for copy in pair:
                copy.wait()
            if b < length // BLOCK:
                for i in range(per_core):
                    here, cols = head_cols(i), columns(False, i, per_core)
                    term = dot_tn(left[block_rows(b), cols], right[block_rows(b), cols])
                    if b == 0:
                        first[here] = term
                    total[here] = term if b == 0 else total[here] + term

    state = jax.ShapeDtypeStruct((width // CORES, D), F32)
    return pl.pallas_call(
        body,
        in_specs=[HBM, HBM],
        out_specs=[VMEM] * 4,
        out_shape=[jax.ShapeDtypeStruct(left.shape, BF16), jax.ShapeDtypeStruct(right.shape, BF16), state, state],
        scratch_shapes=[pltpu.SemaphoreType.DMA((CORES, length // BLOCK, 2))],
        compiler_params=params(12),
        name="bring",
    )(pltpu.with_memory_space_constraint(left, pltpu.HBM), pltpu.with_memory_space_constraint(right, pltpu.HBM))


def products(left, right):
    width = left.shape[1]
    per_core = width // D // CORES

    def body(left, right, first, total):
        for i in range(per_core):
            here, cols = head_cols(i), columns(True, i, per_core)
            one = dot_tn(left[:BLOCK, cols], right[:BLOCK, cols])
            first[here] = one
            total[here] = one + dot_tn(left[BLOCK:, cols], right[BLOCK:, cols])

    state = jax.ShapeDtypeStruct((width // CORES, D), F32)
    return pl.pallas_call(
        body,
        in_specs=[VMEM] * 2,
        out_specs=[VMEM] * 2,
        out_shape=[state, state],
        compiler_params=params(12),
        name="products",
    )(left, right)


def local_attention(q, k, v, is_mine, i, after):
    length, width = q.shape

    def body(q, k, v, _, out, turned):
        cols = columns(is_mine, i, width // D // CORES)
        for c in range(length // BLOCK):
            rows = block_rows(c)
            qv, kv, vv = (x[rows, cols] for x in (q, k, v))
            turned[:, rows] = jnp.transpose(qv)
            a, b, d = lower_product(qv, kv)
            out[c * BLOCK : c * BLOCK + HALF] = dot_nn(a, vv[TOP])
            out[c * BLOCK + HALF : (c + 1) * BLOCK] = dot_nn(beside(b, d), vv)

    return pl.pallas_call(
        body,
        in_specs=[VMEM, VMEM, VMEM, ANY],
        out_specs=[VMEM] * 2,
        out_shape=[jax.ShapeDtypeStruct((length, D), F32), jax.ShapeDtypeStruct((D, length), BF16)],
        compiler_params=params(12),
        cost_estimate=pl.CostEstimate(
            flops=length // BLOCK * 4 * BLOCK * BLOCK * D, bytes_accessed=length * D * 10, transcendentals=0
        ),
        name="local_attention",
    )(q, k, v, after)


def attention_sums(q, grad, local, gain, state, first, is_mine, sums):
    length = q.shape[0]
    per_core = len(local)

    def body(q, grad, *refs):
        local, (gain, state, first, *before, attn, sums) = refs[:per_core], refs[per_core:]
        for c in range(length // BLOCK):
            rows = block_rows(c)
            square = jnp.zeros((BLOCK, D), F32)
            inner = jnp.zeros((BLOCK, D), F32)
            for i in range(per_core):
                cols = columns(is_mine, i, per_core)
                prefix = state[head_cols(i)]
                if c > 0:
                    prefix += first[head_cols(i)]
                a = local[i][rows] + dot_nn(q[rows, cols], prefix.astype(BF16))
                attn[rows, head_cols(i)] = a
                square += a * a
                inner += a * (gain[:, cols] * grad[rows, cols].astype(F32))
            for j, part in enumerate((square, inner)):
                row = jnp.sum(jnp.transpose(part), axis=0, keepdims=True)
                sums[j : j + 1, rows] = row + before[0][j : j + 1, rows] if before else row

    return pl.pallas_call(
        body,
        in_specs=[VMEM] * (5 + per_core + len(sums)),
        out_specs=[VMEM] * 2,
        out_shape=[
            jax.ShapeDtypeStruct((length, per_core * D), F32),
            jax.ShapeDtypeStruct((2, length), F32),
        ],
        compiler_params=params(16),
        name="attention_sums",
    )(q, grad, *local, gain, state, first, *sums)


def gradient(turned, grad, attn, gain, sums, features, is_mine):
    length, width = attn.shape
    per_core = width // D
    blocks = length // BLOCK

    def body(*refs):
        turned, (grad, attn, gain, sums, out, last, total) = refs[:per_core], refs[per_core:]
        for c in range(blocks):
            rows = block_rows(c)
            root = jnp.sqrt(sums[0:1, rows] / features + 1e-05)
            inverse = per_token(1.0 / root)
            weight = per_token(sums[1:2, rows] / (features * root**3))
            for i in range(per_core):
                cols = columns(is_mine, i, per_core)
                scaled = gain[:, cols] * grad[rows, cols].astype(F32)
                g = (scaled * inverse - attn[rows, head_cols(i)] * weight).astype(BF16)
                out[rows, head_cols(i)] = g
                term = dot_nn(turned[i][:, rows], g)
                total[head_cols(i)] = term if c == 0 else total[head_cols(i)] + term
                if c == blocks - 1:
                    last[head_cols(i)] = term

    state = jax.ShapeDtypeStruct((width, D), F32)
    return pl.pallas_call(
        body,
        in_specs=[VMEM] * (4 + per_core),
        out_specs=[VMEM] * 3,
        out_shape=[jax.ShapeDtypeStruct((length, width), BF16), state, state],
        compiler_params=params(16),
        name="gradient",
    )(*turned, grad, attn, gain, sums)


def local_gradients(q, k, v, g, attn, gain, sums, state, first, features, is_mine, i, outs, after):
    length, width = q.shape
    blocks = length // BLOCK
    here = head_cols(i)

    def body(q, k, v, g, attn, gain, sums, state, first, *refs):
        normed, dq, dk, dv, normed_here, dq_here, sems = refs[len(outs) + 1 :]
        cols = columns(is_mine, i, width // D // CORES)
        copies = []

        def send(source, out, j, c):
            copy = pltpu.make_async_copy(source.at[block_rows(c)], out.at[block_rows(c), cols], sems.at[j, c])
            copy.start()
            copies.append(copy)

        for c in range(blocks):
            rows = block_rows(c)
            root = jnp.sqrt(sums[0:1, rows] / features + 1e-05)
            normed_here[rows] = (gain[:, cols] * (attn[rows, here] * per_token(1.0 / root))).astype(BF16)
            send(normed_here, normed, 0, c)
            qv, kv, vv, gv = q[rows, cols], k[rows, cols], v[rows, cols], g[rows, here]
            prefix = state[here] + first[here] if c > 0 else state[here]
            carried = dot_nt(gv, prefix.astype(BF16))
            a, b, d = lower_product(gv, vv)
            top, bottom = slice(c * BLOCK, c * BLOCK + HALF), slice(c * BLOCK + HALF, (c + 1) * BLOCK)
            dq_here[top] = (dot_nn(a, kv[TOP]) + carried[TOP]).astype(BF16)
            dq_here[bottom] = (dot_nn(beside(b, d), kv) + carried[BOTTOM]).astype(BF16)
            send(dq_here, dq, 1, c)
            a, b, d = upper_product(vv, gv)
            dk[top] = dot_nn(beside(a, b), qv)
            dk[bottom] = dot_nn(d, qv[BOTTOM])
            a, b, d = upper_product(kv, qv)
            dv[top] = dot_nn(beside(a, b), gv)
            dv[bottom] = dot_nn(d, gv[BOTTOM])
        for copy in copies:
            copy.wait()

    return pl.pallas_call(
        body,
        in_specs=[VMEM] * 9 + [HBM] * len(outs) + [ANY],
        out_specs=[HBM, HBM, VMEM, VMEM],
        out_shape=[jax.ShapeDtypeStruct((length, width), BF16)] * 2 + [jax.ShapeDtypeStruct((length, D), F32)] * 2,
        scratch_shapes=[pltpu.VMEM((length, D), BF16)] * 2 + [pltpu.SemaphoreType.DMA((2, blocks))],
        input_output_aliases={9 + j: j for j in range(len(outs))},
        compiler_params=params(20),
        cost_estimate=pl.CostEstimate(
            flops=blocks * 12 * BLOCK * BLOCK * D, bytes_accessed=length * D * 20, transcendentals=0
        ),
        name="local_gradients",
    )(q, k, v, g, attn, gain, sums, state, first, *outs, after)


def add_suffix(k, v, dk, dv, state, last, is_mine, outs):
    length, width = k.shape
    per_core = len(dk)
    steps = 2
    part = length // steps

    def body(k, v, *refs):
        dk, dv = refs[:per_core], refs[per_core : 2 * per_core]
        state, last = refs[2 * per_core : 2 * per_core + 2]
        out_k, out_v, here_k, here_v, sems = refs[2 * per_core + 2 + len(outs) :]
        _, _, c = places()
        half = c if is_mine else 1 - c
        target = pl.ds(pl.multiple_of(half * per_core * D, per_core * D), per_core * D)
        copies = []
        for step in range(steps):
            rows = slice(step * part, (step + 1) * part)
            for i in range(per_core):
                cols, here = columns(is_mine, i, per_core), head_cols(i)
                suffix = state[here]
                if step * part < length - BLOCK:
                    suffix += last[here]
                suffix = suffix.astype(BF16)
                here_k[rows, here] = (dk[i][rows] + dot_nt(v[rows, cols], suffix)).astype(BF16)
                here_v[rows, here] = (dv[i][rows] + dot_nn(k[rows, cols], suffix)).astype(BF16)
            for j, (source, out) in enumerate(((here_k, out_k), (here_v, out_v))):
                copy = pltpu.make_async_copy(source.at[rows], out.at[rows, target], sems.at[j, step])
                copy.start()
                copies.append(copy)
        for copy in copies:
            copy.wait()

    shape = jax.ShapeDtypeStruct((length, width), BF16)
    inputs = 4 + 2 * per_core
    return pl.pallas_call(
        body,
        in_specs=[VMEM] * inputs + [HBM] * len(outs),
        out_specs=[HBM, HBM],
        out_shape=[shape, shape],
        scratch_shapes=[pltpu.VMEM((length, per_core * D), BF16)] * 2 + [pltpu.SemaphoreType.DMA((2, steps))],
        input_output_aliases={inputs + j: j for j in range(len(outs))},
        compiler_params=params(16),
        name="add_suffix",
    )(k, v, *dk, *dv, state, last, *outs)


def head_sum(part):
    count = lax.axis_size("head")
    total = part
    for k in range(1, count):
        total = total + lax.ppermute(part, "head", [(i, (i + k) % count) for i in range(count)])
    return total


def on_device(queries, token_keys, values, norm_gain, out_grad):
    heads = queries.shape[1] // D
    features = lax.axis_size("head") * heads * D
    gain = norm_gain.reshape(1, heads * D)
    per_core = heads // CORES
    order = [(is_mine, i) for is_mine in (True, False) for i in range(per_core)]
    keys, vals, first_theirs, theirs = bring(token_keys, values)
    first_mine, mine = products(keys, vals)
    first = {True: first_mine, False: first_theirs}
    local, turned = {True: [], False: []}, {True: [], False: []}

    def attend(is_mine, i):
        def run(after):
            out, query = local_attention(queries, keys, vals, is_mine, i, after)
            local[is_mine].append(out)
            turned[is_mine].append(query)
            return [out]

        return run

    kept, other = entering(mine, theirs, False, [attend(*head) for head in order])
    before = {True: kept, False: other}
    attn, sums = {}, ()
    for is_mine in (True, False):
        attn[is_mine], part = attention_sums(
            queries, out_grad, local[is_mine], gain, before[is_mine], first[is_mine], is_mine, sums
        )
        sums = (part,)
    sums = head_sum(part)
    grad_attn, last, total = {}, {}, {}
    for is_mine in (False, True):
        grad_attn[is_mine], last[is_mine], total[is_mine] = gradient(
            turned[is_mine], out_grad, attn[is_mine], gain, sums, features, is_mine
        )
    outs, key_parts, value_parts = [], {True: [], False: []}, {True: [], False: []}

    def differentiate(is_mine, i):
        def run(after):
            normed, query, key, value = local_gradients(
                queries,
                keys,
                vals,
                grad_attn[is_mine],
                attn[is_mine],
                gain,
                sums,
                before[is_mine],
                first[is_mine],
                features,
                is_mine,
                i,
                tuple(outs),
                after,
            )
            outs[:] = [normed, query]
            key_parts[is_mine].append(key)
            value_parts[is_mine].append(value)
            return [value]

        return run

    kept, other = entering(total[True], total[False], True, [differentiate(*head) for head in order])
    normed_out, grad_query = outs
    outs = ()
    for is_mine, state in ((True, kept), (False, other)):
        outs = add_suffix(keys, vals, key_parts[is_mine], value_parts[is_mine], state, last[is_mine], is_mine, outs)
    grad_key, grad_value = outs
    return normed_out, grad_query, grad_key, grad_value


def solution(mesh):
    placed = (P("seq", "head"), P("seq", "head"), P("seq", "head"), P("head"), P("seq", "head"))
    return jax.shard_map(
        on_device,
        mesh=mesh,
        in_specs=placed,
        out_specs=(P("seq", "head"), P("seq", "head"), P("seq", "head"), P("seq", "head")),
        check_vma=False,
    )
```
